32 devices in a mesh: rows: 8 (over z, y), seq: 4 (over x, core).
Axes of the slice: x: 2, y: 2, z: 4, core: 2. Of those that a mesh axis runs over, the one named last changes fastest.
Arguments:
- tokens: bfloat16 [16, 1024, 1024], P('rows', 'seq'), may hold values from -6 to 6
- bounds: int32 [16, 4], P('rows'), may hold values from 0 to 1023, as said below
- norm1_gain: float32 [1024], replicated, may hold values from 0.25 to 1.75
- norm1_bias: float32 [1024], replicated, may hold values from -1.5 to 1.5
- w_qkv: bfloat16 [1024, 3072], replicated, may hold values from -0.1875 to 0.1875
- w_proj: bfloat16 [1024, 1024], replicated, may hold values from -1.5 to 1.5
- norm2_gain: float32 [1024], replicated, may hold values from 0.25 to 1.75
- norm2_bias: float32 [1024], replicated, may hold values from -1.5 to 1.5
- w_up: bfloat16 [1024, 4096], replicated, may hold values from -0.1875 to 0.1875
- up_bias: float32 [4096], replicated, may hold values from -1.5 to 1.5
- w_down: bfloat16 [4096, 1024], replicated, may hold values from -0.09375 to 0.09375
- down_bias: float32 [1024], replicated, may hold values from -1.5 to 1.5
- cotangent: bfloat16 [16, 1024, 1024], P('rows', 'seq'), may hold values from -6 to 6
Outputs:
- layer_out: bfloat16 [16, 1024, 1024], P('rows', 'seq')
- grad_tokens: float32 [16, 1024, 1024], P('rows', 'seq')
- grad_norm1_gain: float32 [1024], P(('rows', 'seq'))
- grad_norm1_bias: float32 [1024], P(('rows', 'seq'))
- grad_qkv: float32 [1024, 3072], P(('rows', 'seq'))
- grad_proj: float32 [1024, 1024], P(('rows', 'seq'))
- grad_norm2_gain: float32 [1024], P(('rows', 'seq'))
- grad_norm2_bias: float32 [1024], P(('rows', 'seq'))
- grad_up: float32 [1024, 4096], P(('rows', 'seq'))
- grad_up_bias: float32 [4096], P(('rows', 'seq'))
- grad_down: float32 [4096, 1024], P(('rows', 'seq'))
- grad_down_bias: float32 [1024], P(('rows', 'seq'))
The draws below stay inside these ranges and needn't reach their ends.
Inputs may be any that keep to these rules, and one draw needn't show every extreme that they name: `bounds`: each row lists the first positions of its 4 documents in increasing order, the first being 0. In every aligned block of 2 rows one row has a document that begins within its first 256 positions and ends within its last 256.
All inputs are finite; a program needn't handle non-finite values.
Results may differ from the reference program's by a relative error of at most 0.007.
Values may be sent and summed in bfloat16 or wider, within the bound.
No kernel may reach another device: no remote copies, remote signals or barrier semaphores. Data moves between devices by JAX's collectives and lax.ppermute only.
A program may use at most 256 MiB of HBM per device.

```python
import jax
import jax.numpy as jnp
from jax import lax

D = 1024
HEADS = 16
FF = 4096
STRETCH = 256
ROWS_DEV = 2
ROWS = 16
LENGTH = 1024
N_SEQ = 4


def draw_bounds(key, part):
    key = jax.random.fold_in(key, 11)
    key_free, key_a, key_b, key_row = jax.random.split(key, 4)
    row_keys = jax.random.split(key_free, ROWS)

    def pick(row_key):
        return jnp.sort(jax.random.permutation(row_key, LENGTH - 1)[:3] + 1)
    spread_starts = jax.vmap(pick)(row_keys).astype(jnp.int32)
    first_start = jax.random.randint(key_a, (ROWS,), 1, STRETCH // 2 + 1)
    second_start = jax.random.randint(key_b, (ROWS,), LENGTH - STRETCH // 2, LENGTH - 1)
    final_start = jnp.full((ROWS,), LENGTH - 1, jnp.int32)
    long_starts = jnp.stack([first_start, second_start, final_start], 1).astype(jnp.int32)
    chosen = jax.random.randint(key_row, (ROWS // ROWS_DEV,), 0, ROWS_DEV)
    is_long = jnp.arange(ROWS) % ROWS_DEV == jnp.repeat(chosen, ROWS_DEV)
    rest = jnp.where(is_long[:, None], long_starts, spread_starts)
    return jnp.concatenate([jnp.zeros((ROWS, 1), jnp.int32), rest], 1).astype(jnp.int32)


def level_of(own_key, shape, cuts, low, largest):
    level, own = 1.0, jax.random.fold_in(own_key, 6)
    for dim, blocks in cuts:
        draws = jnp.exp(jax.random.uniform(jax.random.fold_in(own, dim), (blocks,), jnp.float32, low / len(cuts), largest / len(cuts)))
        level = level * jnp.repeat(draws, shape[dim] // blocks).reshape([-1 if axis == dim else 1 for axis in range(len(shape))])
    return level


def scatter_about(own_key, extent, scale, most, cuts=(), kind=jnp.bfloat16):
    factor_of = level_of(own_key, extent, cuts, -0.22, 0.18) if cuts else 1.0
    array = jax.random.normal(own_key, extent, jnp.float32) * scale * factor_of
    return jnp.minimum(jnp.maximum(array, -most), most).astype(kind)


def setup_inputs(seed: int = 0) -> dict:
    keys = jax.random.split(jax.random.key(seed), 14)
    tokens = scatter_about(keys[0], (ROWS, LENGTH, D), 1.0, 6.0, ((0, 8), (1, 4)))
    bounds = draw_bounds(jax.random.fold_in(keys[13], 71), 0)
    norm1_gain = jnp.clip(1.0 + 0.15 * jax.random.normal(keys[2], (D,), jnp.float32), 0.25, 1.75)
    norm1_bias = scatter_about(keys[3], (D,), 0.3, 1.5, (), jnp.float32)
    w_qkv = scatter_about(keys[4], (D, 3 * D), D ** -0.5, 0.1875)
    w_proj = scatter_about(keys[5], (D, D), (max(D // 64, 1)) ** -0.5, 1.5)
    norm2_gain = jnp.clip(1.0 + 0.15 * jax.random.normal(keys[6], (D,), jnp.float32), 0.25, 1.75)
    norm2_bias = scatter_about(keys[7], (D,), 0.3, 1.5, (), jnp.float32)
    w_up = scatter_about(keys[8], (D, FF), D ** -0.5, 0.1875)
    up_bias = scatter_about(keys[9], (FF,), 0.3, 1.5, (), jnp.float32)
    w_down = scatter_about(keys[10], (FF, D), FF ** -0.5, 0.09375)
    down_bias = scatter_about(keys[11], (D,), 0.3, 1.5, (), jnp.float32)
    cotangent = scatter_about(keys[12], (ROWS, LENGTH, D), 1.0, 6.0, ((0, 8), (1, 4)))
    return dict(tokens=tokens, bounds=bounds, norm1_gain=norm1_gain, norm1_bias=norm1_bias, w_qkv=w_qkv, w_proj=w_proj, norm2_gain=norm2_gain, norm2_bias=norm2_bias, w_up=w_up, up_bias=up_bias, w_down=w_down, down_bias=down_bias, cotangent=cotangent)


EPS = 1e-05
HIGH = lax.Precision.HIGHEST

@jax.custom_vjp
def low(v):
    return lax.optimization_barrier(v.astype(jnp.bfloat16)).astype(jnp.float32)

@jax.custom_vjp
def low_back(v):
    return v

def low_keep(v):
    return (low(v), None)

def low_pass(kept, grad):
    return (grad,)

def back_keep(v):
    return (v, None)

def back_low(kept, grad):
    return (low(grad),)
low.defvjp(low_keep, low_pass)
low_back.defvjp(back_keep, back_low)

def layer_norm(inputs, gain, bias):
    center = inputs - lax.optimization_barrier(jnp.mean(inputs, -1, keepdims=True))
    spread = lax.optimization_barrier(jnp.mean(center * center, -1, keepdims=True))
    return center * lax.rsqrt(spread + EPS) * gain + bias

def row_forward(params, x_row, starts):
    gain1, bias1, w_qkv, w_proj, gain2, bias2, w_up, up_bias, w_down, down_bias = params
    length = x_row.shape[0]
    model = x_row.shape[1]
    head = model // HEADS
    normed = low(layer_norm(x_row, gain1, bias1))
    mixed = low_back(jnp.dot(normed, w_qkv, precision=HIGH))
    query_map = low(jax.nn.elu(mixed[:, :model]) + 1.0).reshape(N_SEQ, STRETCH, HEADS, head)
    key_map = low(jax.nn.elu(mixed[:, model:2 * model]) + 1.0).reshape(N_SEQ, STRETCH, HEADS, head)
    values = low(mixed[:, 2 * model:]).reshape(N_SEQ, STRETCH, HEADS, head)
    place = jnp.arange(length, dtype=jnp.int32)
    docs = (lax.optimization_barrier(jnp.sum((starts[None, :] <= place[:, None]).astype(jnp.int32), 1)) - 1).astype(jnp.int32)
    docs = docs.reshape(N_SEQ, STRETCH)
    firsts = jnp.arange(N_SEQ, dtype=jnp.int32) * STRETCH
    befores = (lax.optimization_barrier(jnp.sum((starts[None, :] <= firsts[:, None] - 1).astype(jnp.int32), 1)) - 1).astype(jnp.int32)
    causal = jnp.arange(STRETCH)[:, None] >= jnp.arange(STRETCH)[None, :]

    def block(carry, item):
        state, state_sum = carry
        block_q, block_k, block_v, block_docs, before = item
        scores = jnp.einsum('the,she->hts', block_q, block_k, precision=HIGH)
        mask = (causal & (block_docs[:, None] == block_docs[None, :])).astype(jnp.float32)[None]
        weights = low(low_back(scores * mask))
        carried = (block_docs == before).astype(jnp.float32)
        numer = jnp.einsum('hts,she->the', weights, block_v, precision=HIGH)
        numer = numer + carried[:, None, None] * jnp.einsum('the,hef->thf', block_q, state, precision=HIGH)
        numer = low_back(numer)
        denom = lax.optimization_barrier(jnp.sum(weights, -1)).T + carried[:, None] * jnp.einsum('the,he->th', block_q, state_sum, precision=HIGH)
        outputs = numer / denom[:, :, None]
        keep = (block_docs == block_docs[-1]).astype(jnp.float32)[:, None, None]
        own = jnp.einsum('she,shf->hef', block_k * keep, block_v, precision=HIGH)
        own_sum = lax.optimization_barrier(jnp.sum(block_k * keep, 0))
        flag = (block_docs[-1] != before).astype(jnp.float32)
        return ((own + (1.0 - flag) * state, own_sum + (1.0 - flag) * state_sum), outputs)
    start = (jnp.zeros((HEADS, head, head), jnp.float32), jnp.zeros((HEADS, head), jnp.float32))
    unused, outputs = lax.scan(jax.checkpoint(block), start, (query_map, key_map, values, docs, befores))
    attended = low(outputs.reshape(length, model))
    middle = x_row + low_back(jnp.dot(attended, w_proj, precision=HIGH))
    normed2 = low(layer_norm(middle, gain2, bias2))
    hidden = low(jax.nn.gelu(low_back(jnp.dot(normed2, w_up, precision=HIGH) + up_bias)))
    return middle + low_back(jnp.dot(hidden, w_down, precision=HIGH) + down_bias)

def reference(tokens, bounds, norm1_gain, norm1_bias, w_qkv, w_proj, norm2_gain, norm2_bias, w_up, up_bias, w_down, down_bias, cotangent):
    params = tuple((p.astype(jnp.float32) for p in (norm1_gain, norm1_bias, w_qkv, w_proj, norm2_gain, norm2_bias, w_up, up_bias, w_down, down_bias)))
    inputs = tokens.astype(jnp.float32)

    def forward(x_all, weights):
        return lax.map(lambda item: row_forward(weights, item[0], item[1]), (x_all, bounds))
    result, pull = jax.vjp(forward, inputs, params)
    grad_x, grads = pull(cotangent.astype(jnp.float32))
    g_gain1, g_bias1, g_qkv, g_proj, g_gain2, g_bias2, g_up, g_upb, g_down, g_downb = grads
    return (result.astype(jnp.bfloat16), grad_x, g_gain1, g_bias1, g_qkv, g_proj, g_gain2, g_bias2, g_up, g_upb, g_down, g_downb)
```

```python
import functools

import jax
import jax.numpy as jnp
from jax import lax
from jax.experimental import pallas as pl
from jax.experimental.pallas import tpu as pltpu
from jax.sharding import PartitionSpec as P

HEADS = 16
EPS = 1e-05
BF, F32 = jnp.bfloat16, jnp.float32
AXES = ("rows", "seq")
SUMS = 64
DEPTH = 80
TILE = 512


def dot(a, b):
    return jnp.dot(a, b, preferred_element_type=F32)


def dot_nt(a, b):
    return lax.dot_general(a, b, (((1,), (1,)), ((), ())), preferred_element_type=F32)


def dot_tn(a, b):
    return lax.dot_general(a, b, (((0,), (0,)), ((), ())), preferred_element_type=F32)


def iota(shape, dim):
    return lax.broadcasted_iota(jnp.int32, shape, dim)


def full(shape):
    zeros = (0,) * len(shape)
    return pl.BlockSpec(shape, lambda *unused: zeros)


SMEM = pl.BlockSpec(memory_space=pltpu.SMEM)


def kernel_call(body, args, specs, outs, out_specs, grid, scratch=(), after=(), flops=0, table=None):
    lead = 0 if table is None else 1
    n_in, n_after = lead + len(args), len(after)

    def wrapped(*refs):
        body(*refs[:n_in], *refs[n_in + n_after :])

    shapes = [jax.ShapeDtypeStruct(s, d) for s, d in outs]
    moved = sum(a.size * a.dtype.itemsize for a in args)
    moved += sum(s.size * s.dtype.itemsize for s in shapes)
    every = [*specs, *[pl.BlockSpec(memory_space=pl.ANY)] * n_after]
    common = dict(
        out_shape=shapes,
        compiler_params=pltpu.CompilerParams(vmem_limit_bytes=50 << 20),
        cost_estimate=pl.CostEstimate(flops=flops, bytes_accessed=moved, transcendentals=0),
    )
    if table is None:
        run = pl.pallas_call(
            wrapped, grid=grid, in_specs=every, out_specs=out_specs, scratch_shapes=scratch, **common
        )
        return run(*args, *after)
    spec = pltpu.PrefetchScalarGridSpec(
        num_scalar_prefetch=1, grid=grid, in_specs=every, out_specs=out_specs, scratch_shapes=scratch
    )
    return pl.pallas_call(wrapped, grid_spec=spec, **common)(table, *args, *after)


def normal(x):
    center = x - jnp.mean(x, -1, keepdims=True)
    root = lax.rsqrt(jnp.mean(center * center, -1, keepdims=True) + EPS)
    return center * root, root


def norm_grad(e, x, gain):
    hat, root = normal(x)
    g = e * gain
    back = root * (g - jnp.mean(g, -1, keepdims=True) - hat * jnp.mean(g * hat, -1, keepdims=True))
    return back, jnp.sum(e * hat, 0, keepdims=True), jnp.sum(e, 0, keepdims=True)


def feature(u):
    return jnp.where(u > 0, u + 1.0, jnp.exp(jnp.minimum(u, 0.0)))


def keep_from(lb, row, span):
    last = 0 - span
    for k in range(lb.shape[1]):
        last = jnp.where(lb[row, k] < span, jnp.maximum(last, lb[row, k]), last)
    return last


def carry_to(lb, row, span):
    end = span
    for k in range(lb.shape[1]):
        end = jnp.where(lb[row, k] >= 0, jnp.minimum(end, lb[row, k]), end)
    return end


def block_mask(lb, row, span):
    t, s = iota((span, span), 0), iota((span, span), 1)
    ok = s <= t
    for k in range(lb.shape[1]):
        ok = ok & ((lb[row, k] > t) | (s >= lb[row, k]))
    return ok.astype(F32)


def pack_state(m):
    half = m.shape[0] // 2
    return jnp.where(iota((half, m.shape[1]), 1) < half, m[:half], m[half:])


def unpack_state(c):
    half = c.shape[0]
    left = iota(c.shape, 1) < half
    return jnp.concatenate([jnp.where(left, c, 0.0), jnp.where(left, 0.0, c)], 0)


def split(x):
    hi = x.astype(BF)
    return hi, (x - hi.astype(F32)).astype(BF)


def head_ones(lanes=128):
    half = lanes // 2
    return ((iota((lanes, lanes), 0) < half) == (iota((lanes, lanes), 1) < half)).astype(BF)


def head_sum(x):
    hi, lo = split(x)
    ones = head_ones(x.shape[1])
    return dot(jnp.concatenate([hi, lo], 1), jnp.concatenate([ones, ones], 0))


def dot_split(a, m):
    hi, lo = split(m)
    return dot(jnp.concatenate([a, a], 1), jnp.concatenate([hi, lo], 0))


def keys_values(lb, tokens, gain, bias, w_qkv, span, after=()):
    count, model = tokens.shape
    rows, width = count // span, 256

    def body(lb, x, g, b, wk, wv, n1, km, v, own):
        @pl.when(pl.program_id(0) == 0)
        def _():
            n1[...] = (normal(x[...].astype(F32))[0] * g[...] + b[...]).astype(BF)

        n = n1[...]
        key = feature(dot(n, wk[...])).astype(BF)
        val = dot(n, wv[...]).astype(BF)
        km[...], v[...] = key, val
        for r in range(rows):
            part = slice(r * span, (r + 1) * span)
            kept = iota((span, width), 0) >= keep_from(lb, r, span)
            owned = jnp.where(kept, key[part], jnp.zeros((), BF))
            for p in range(width // 128):
                lanes = slice(p * 128, (p + 1) * 128)
                m = dot_tn(owned[:, lanes], val[part, lanes])
                own[r, p, 0:SUMS] = pack_state(m).astype(BF)
                total = jnp.sum(owned[:, lanes].astype(F32), 0, keepdims=True)
                own[r, p, SUMS:DEPTH] = jnp.broadcast_to(total, (DEPTH - SUMS, 128)).astype(BF)

    steps = model // width
    tile = pl.BlockSpec((count, width), lambda j: (0, j))
    return kernel_call(
        body,
        (lb, tokens, gain, bias, w_qkv, w_qkv),
        [
            SMEM,
            full((count, model)),
            full((1, model)),
            full((1, model)),
            pl.BlockSpec((model, width), lambda j: (0, steps + j)),
            pl.BlockSpec((model, width), lambda j: (0, 2 * steps + j)),
        ],
        [
            ((count, model), BF),
            ((count, model), BF),
            ((count, model), BF),
            ((rows, model // 128, DEPTH, 128), BF),
        ],
        [
            full((count, model)),
            tile,
            tile,
            pl.BlockSpec((rows, width // 128, DEPTH, 128), lambda j: (0, j, 0, 0)),
        ],
        (steps,),
        after=after,
        flops=4 * count * model * model,
    )


def queries(normed, w_qkv, after=()):
    count, model = normed.shape

    def body(n, w, q):
        q[...] = feature(dot(n[...], w[...])).astype(BF)

    tile = pl.BlockSpec((count, TILE), lambda j: (0, j))
    return kernel_call(
        body,
        (normed, w_qkv),
        [full((count, model)), pl.BlockSpec((model, TILE), lambda j: (0, j))],
        [((count, model), BF)],
        [tile],
        (model // TILE,),
        after=after,
        flops=2 * count * model * model,
    )[0]


def active_grads(cotangent, w_down, after=()):
    count, model = cotangent.shape
    ff = w_down.shape[0]

    def body(c, w, out):
        out[...] = dot_nt(c[...], w[...])

    return kernel_call(
        body,
        (cotangent, w_down),
        [full((count, model)), pl.BlockSpec((TILE, model), lambda j: (j, 0))],
        [((count, ff), F32)],
        [pl.BlockSpec((count, TILE), lambda j: (0, j))],
        (ff // TILE,),
        after=after,
        flops=2 * count * model * ff,
    )[0]


def attend_inside(lb, query, key, values, span, after=()):
    count, model = query.shape
    width = 512

    def body(lb, q_ref, k_ref, v_ref, numer, denom, mask):
        row = pl.program_id(0)

        @pl.when(pl.program_id(1) == 0)
        def _():
            mask[...] = block_mask(lb, row, span)

        left = iota((span, 128), 1) < 64
        zero = jnp.zeros((), BF)
        for p in range(width // 128):
            lanes = slice(p * 128, (p + 1) * 128)
            q, k, v = q_ref[:, lanes], k_ref[:, lanes], v_ref[:, lanes]
            total = 0.0
            for e in range(2):
                mine = left if e == 0 else ~left
                scores = dot_nt(jnp.where(mine, q, zero), k)
                weights = (scores * mask[...]).astype(BF)
                both = jnp.concatenate([jnp.where(mine, v, zero), mine.astype(BF)], 1)
                total = total + dot(weights, both)
            numer[:, lanes] = total[:, :128]
            denom[:, lanes] = total[:, 128:]

    tile = pl.BlockSpec((span, width), lambda r, h: (r, h))
    return kernel_call(
        body,
        (lb, query, key, values),
        [SMEM, tile, tile, tile],
        [((count, model), F32)] * 2,
        [tile, tile],
        (count // span, model // width),
        scratch=[pltpu.VMEM((span, span), F32)],
        after=after,
        flops=16 * count * span * model // 4,
    )


def attend_join(lb, state, query, numer, denom, tokens, w_proj, gain, bias, span, after=()):
    count, model = query.shape
    step = 128
    pairs = model // 128

    def body(lb, st, q_ref, num_ref, den_ref, x, w, g, b, att, rden, middle, n2):
        i = pl.program_id(0)
        row = i * step // span
        place = iota((step, 128), 0) + lax.rem(i * step, span)
        carried = place < carry_to(lb, row, span)
        for p in range(pairs):
            lanes = slice(p * 128, (p + 1) * 128)
            q = jnp.where(carried, q_ref[:, lanes], jnp.zeros((), BF))
            num = num_ref[:, lanes] + dot_split(q, unpack_state(st[0, p, 0:SUMS]))
            den = den_ref[:, lanes] + head_sum(q.astype(F32) * st[0, p, SUMS : SUMS + 1])
            inv = 1.0 / den
            rden[:, lanes] = inv
            att[:, lanes] = (num * inv).astype(BF)
        mid = x[...].astype(F32) + dot(att[...], w[...])
        middle[...] = mid
        n2[...] = (normal(mid)[0] * g[...] + b[...]).astype(BF)

    tile = pl.BlockSpec((step, model), lambda i: (i, 0))
    return kernel_call(
        body,
        (lb, state, query, numer, denom, tokens, w_proj, gain, bias),
        [
            SMEM,
            pl.BlockSpec((1, pairs, DEPTH, 128), lambda i: (i * step // span, 0, 0, 0)),
            tile,
            tile,
            tile,
            tile,
            full(w_proj.shape),
            full((1, model)),
            full((1, model)),
        ],
        [((count, model), BF), ((count, model), F32), ((count, model), F32), ((count, model), BF)],
        [tile] * 4,
        (count // step,),
        after=after,
        flops=2 * count * model * (model + 512),
    )


def expand(normed, w_up, up_bias, d_active, after=()):
    count, model = normed.shape
    ff = w_up.shape[1]
    c0, c1 = 0.7978845608028654, 0.7978845608028654 * 0.044715

    def body(n, w, b, da, hid, hid_t, dp, total):
        for part in range(2):
            rows = slice(part * count // 2, (part + 1) * count // 2)
            u = dot(n[rows, :], w[...]) + b[...]
            sq = u * u
            t = jnp.tanh(u * (c0 + c1 * sq))
            half = 0.5 * u
            h = (half + half * t).astype(BF)
            hid[rows, :] = h
            hid_t[:, rows] = h.T
            slope = (0.5 + 0.5 * t) + half * (1.0 - t * t) * (c0 + 3.0 * c1 * sq)
            d = (slope * da[rows, :]).astype(BF)
            dp[rows, :] = d
            part_sum = jnp.sum(d.astype(F32), 0, keepdims=True)
            total[...] = part_sum if part == 0 else total[...] + part_sum

    tile = pl.BlockSpec((count, TILE), lambda j: (0, j))
    vec = pl.BlockSpec((1, TILE), lambda j: (0, j))
    return kernel_call(
        body,
        (normed, w_up, up_bias, d_active),
        [full((count, model)), pl.BlockSpec((model, TILE), lambda j: (0, j)), vec, tile],
        [((count, ff), BF), ((ff, count), BF), ((count, ff), BF), ((1, ff), F32)],
        [tile, pl.BlockSpec((TILE, count), lambda j: (j, 0)), tile, vec],
        (ff // TILE,),
        after=after,
        flops=2 * count * model * ff,
    )


def turned(x, place, shards, after=()):
    count, model = x.shape
    deep = model // shards

    def body(place, x, out):
        for j in range(model // 128):
            t = x[:, j * 128 : (j + 1) * 128].T
            for k in range(128 // deep):
                at = pl.multiple_of(place[j * (128 // deep) + k] * deep, deep)
                out[pl.ds(at, deep), :] = t[k * deep : (k + 1) * deep]

    return kernel_call(
        body, (place, x), [SMEM, full(x.shape)], [((model, count), BF)], [full((model, count))], (1,), after=after
    )[0]


def weight_grad(lhs_t, rhs, block_of, steps, table, got=None, after=()):
    deep, count = lhs_t.shape
    half = deep // 2
    block = (*(None,) * (rhs.ndim - 2), count, TILE)
    in_specs = [full(lhs_t.shape), pl.BlockSpec(block, lambda j, t: block_of(j, t))]
    flops = 2 * deep * count * TILE * steps
    if got is None:

        shards = table.shape[0] - 1
        rows = deep // shards

        def body(table, a, b, out):
            total = dot(a[...], b[...]).astype(BF)
            for j in range(shards):
                at = (j & 0b01010) | (j >> 4 & 1) << 2 | (j >> 2 & 1) << 4 | (~j & 1)
                out[at * rows : (at + 1) * rows, :] = total[j * rows : (j + 1) * rows]

        return kernel_call(
            body,
            (lhs_t, rhs),
            in_specs,
            [((deep, TILE * steps), BF)],
            [pl.BlockSpec((deep, TILE), lambda j, t: (0, j))],
            (steps,),
            after=after,
            flops=flops,
            table=table,
        )[0]

    def body(table, a, b, g, send, keep):
        total = dot(a[...], b[...]) + g[...].astype(F32)
        send[...] = total[:half].astype(BF)
        keep[...] = total[half:].astype(BF)

    return kernel_call(
        body,
        (lhs_t, rhs, got),
        [*in_specs, pl.BlockSpec((deep, TILE), lambda j, t: (0, j))],
        [((half, TILE * steps), BF)] * 2,
        [pl.BlockSpec((half, TILE), lambda j, t: (0, j))] * 2,
        (steps,),
        after=after,
        flops=flops,
        table=table,
    )


def down_grad(hidden_t, cotangent, width, column_of, table, got=None, after=()):
    ff, count = hidden_t.shape
    shards = table.shape[0] - 1
    deep = ff // shards
    per = TILE // deep
    steps = ff // TILE
    half = steps // 2

    def piece(k):
        return pl.BlockSpec((deep, count), lambda i, t: (t[per * i + k], 0))

    in_specs = [piece(k) for k in range(per)]
    in_specs += [pl.BlockSpec((count, width), lambda i, t: (0, column_of(t)))]
    args = (*[hidden_t] * per, cotangent)
    flops = 2 * ff * count * width

    def product(refs):
        return dot(jnp.concatenate([r[...] for r in refs[:per]], 0), refs[per][...])

    if got is None:

        def body(table, *refs):
            refs[-1][...] = product(refs).astype(BF)

        return kernel_call(
            body,
            args,
            in_specs,
            [((ff, width), BF)],
            [pl.BlockSpec((TILE, width), lambda i, t: (i, 0))],
            (steps,),
            after=after,
            flops=flops,
            table=table,
        )[0]

    def body(table, *refs):
        g, send, keep = refs[per + 1 :]
        total = (product(refs) + g[...].astype(F32)).astype(BF)

        @pl.when(pl.program_id(0) < half)
        def _():
            send[...] = total

        @pl.when(pl.program_id(0) >= half)
        def _():
            keep[...] = total

    return kernel_call(
        body,
        (*args, got),
        [*in_specs, pl.BlockSpec((TILE, width), lambda i, t: (i, 0))],
        [((ff // 2, width), BF)] * 2,
        [
            pl.BlockSpec((TILE, width), lambda i, t: (jnp.minimum(i, half - 1), 0)),
            pl.BlockSpec((TILE, width), lambda i, t: (jnp.maximum(i - half, 0), 0)),
        ],
        (steps,),
        after=after,
        flops=flops,
        table=table,
    )


def second_norm_grads(d_pre, w_up, middle, cotangent, gain, after=()):
    count, ff = d_pre.shape
    model = w_up.shape[0]
    steps = ff // TILE

    def body(d, w, mid, cot, g, d_mid, branch, g_gain, g_bias, g_down, total):
        j = pl.program_id(0)

        @pl.when(j == 0)
        def _():
            total[...] = dot_nt(d[...], w[...])

        @pl.when(j > 0)
        def _():
            total[...] += dot_nt(d[...], w[...])

        @pl.when(j == steps - 1)
        def _():
            back, g_gain[...], g_bias[...] = norm_grad(total[...], mid[...], g[...])
            c = cot[...].astype(F32)
            g_down[...] = jnp.sum(c, 0, keepdims=True)
            out = c + back
            d_mid[...] = out
            branch[...] = out.astype(BF)

    vec = ((1, model), F32)
    return kernel_call(
        body,
        (d_pre, w_up, middle, cotangent, gain),
        [
            pl.BlockSpec((count, TILE), lambda j: (0, j)),
            pl.BlockSpec((model, TILE), lambda j: (0, j)),
            full((count, model)),
            full((count, model)),
            full((1, model)),
        ],
        [((count, model), F32), ((count, model), BF), vec, vec, vec],
        [full((count, model)), full((count, model)), *[full((1, model))] * 3],
        (steps,),
        scratch=[pltpu.VMEM((count, model), F32)],
        after=after,
        flops=2 * count * model * ff,
    )


def mixer_grads(lb, branch, w_proj, attended, rden, query, span, after=()):
    count, model = branch.shape
    rows, pairs = count // span, model // 128

    def body(lb, br, w, att, rd, q_ref, dn, dd, own):
        d_att = dot_nt(br[...], w[...])
        carried = iota((span, 128), 0) < carry_to(lb, pl.program_id(0), span)
        for p in range(pairs):
            lanes = slice(p * 128, (p + 1) * 128)
            d, inv = d_att[:, lanes], rd[:, lanes]
            d_den = -head_sum(d * att[:, lanes].astype(F32)) * inv
            d_num = (d * inv).astype(BF)
            dn[:, lanes], dd[:, lanes] = d_num, d_den
            q = jnp.where(carried, q_ref[:, lanes], jnp.zeros((), BF))
            own[0, p, 0:SUMS] = pack_state(dot_tn(q, d_num)).astype(BF)
            total = jnp.sum(d_den * q.astype(F32), 0, keepdims=True)
            own[0, p, SUMS:DEPTH] = jnp.broadcast_to(total, (DEPTH - SUMS, 128)).astype(BF)

    tile = pl.BlockSpec((span, model), lambda r: (r, 0))
    return kernel_call(
        body,
        (lb, branch, w_proj, attended, rden, query),
        [SMEM, tile, full(w_proj.shape), tile, tile, tile],
        [((count, model), BF), ((count, model), F32), ((rows, pairs, DEPTH, 128), BF)],
        [tile, tile, pl.BlockSpec((1, pairs, DEPTH, 128), lambda r: (r, 0, 0, 0))],
        (rows,),
        after=after,
        flops=2 * count * model * (model + 512),
    )


def attend_back(lb, query, key, values, d_num, d_den, state, d_own, span, after=()):
    count, model = query.shape
    width = 512
    half = width // 128

    def body(lb, q_ref, k_ref, v_ref, dn_ref, dd_ref, st, own, out, mask, mask_t):
        row = pl.program_id(0)

        @pl.when(pl.program_id(1) == 0)
        def _():
            m = block_mask(lb, row, span)
            mask[...] = m
            mask_t[...] = m.T

        lane = iota((span, 128), 1)
        left = lane < 64
        place = iota((span, 128), 0)
        carried = place < carry_to(lb, row, span)
        kept = place >= keep_from(lb, row, span)
        zero = jnp.zeros((), BF)
        for p in range(half):
            lanes = slice(p * 128, (p + 1) * 128)
            q, k, v = q_ref[:, lanes], k_ref[:, lanes], v_ref[:, lanes]
            dn, dd = dn_ref[:, lanes], dd_ref[:, lanes]
            hi, lo = split(dd)
            v_ones = jnp.concatenate([v, jnp.ones_like(v)], 1)
            dq = dk = dv = 0.0
            for e in range(2):
                mine = left if e == 0 else ~left
                at = 64 * e
                qm, dnm = jnp.where(mine, q, zero), jnp.where(mine, dn, zero)
                extra = jnp.where(lane == at, hi, jnp.where(lane == at + 1, lo, zero))
                dn_den = jnp.concatenate([dnm, extra], 1)
                ds = (dot_nt(dn_den, v_ones).astype(BF).astype(F32) * mask[...]).astype(BF)
                ds_t = (dot_nt(v_ones, dn_den).astype(BF).astype(F32) * mask_t[...]).astype(BF)
                w_t = (dot_nt(k, qm) * mask_t[...]).astype(BF)
                dq = dq + dot(ds, jnp.where(mine, k, zero))
                dk = dk + dot(ds_t, qm)
                dv = dv + dot(w_t, dnm)
            s = unpack_state(st[0, p, 0:SUMS])
            o = unpack_state(own[0, p, 0:SUMS])
            s_hi, s_lo = split(s)
            o_hi, o_lo = split(o)
            through_s = dot_nt(jnp.concatenate([dn, dn], 1), jnp.concatenate([s_hi, s_lo], 1))
            through_o = dot_nt(jnp.concatenate([v, v], 1), jnp.concatenate([o_hi, o_lo], 1))
            dq = dq + jnp.where(carried, through_s + dd * st[0, p, SUMS : SUMS + 1], 0.0)
            dk = dk + jnp.where(kept, through_o + own[0, p, SUMS : SUMS + 1], 0.0)
            dv = dv + jnp.where(kept, dot(jnp.concatenate([k, k], 1), jnp.concatenate([o_hi, o_lo], 0)), 0.0)
            out[0, :, lanes] = (dq * jnp.minimum(q.astype(F32), 1.0)).astype(BF)
            out[1, :, lanes] = (dk * jnp.minimum(k.astype(F32), 1.0)).astype(BF)
            out[2, :, lanes] = dv.astype(BF)

    tile = pl.BlockSpec((span, width), lambda r, h: (r, h))
    states = pl.BlockSpec((1, half, DEPTH, 128), lambda r, h: (r, h, 0, 0))
    return kernel_call(
        body,
        (lb, query, key, values, d_num, d_den, state, d_own),
        [SMEM, tile, tile, tile, tile, tile, states, states],
        [((3, count, model), BF)],
        [pl.BlockSpec((3, span, width), lambda r, h: (0, r, h))],
        (count // span, model // width),
        scratch=[pltpu.VMEM((span, span), F32)] * 2,
        after=after,
        flops=32 * count * span * model // 4,
    )[0]


def first_norm_grads(d_mixed, w_qkv, tokens, d_middle, gain, after=()):
    parts, count, model = d_mixed.shape
    steps = parts * model // TILE
    per = model // TILE

    def body(d, w, x, dm, g, out, g_gain, g_bias, total):
        j = pl.program_id(0)

        @pl.when(j == 0)
        def _():
            total[...] = dot_nt(d[...], w[...])

        @pl.when(j > 0)
        def _():
            total[...] += dot_nt(d[...], w[...])

        @pl.when(j == steps - 1)
        def _():
            back, g_gain[...], g_bias[...] = norm_grad(total[...], x[...].astype(F32), g[...])
            out[...] = dm[...] + back

    vec = ((1, model), F32)
    return kernel_call(
        body,
        (d_mixed, w_qkv, tokens, d_middle, gain),
        [
            pl.BlockSpec((None, count, TILE), lambda j: (j // per, 0, lax.rem(j, per))),
            pl.BlockSpec((model, TILE), lambda j: (0, j)),
            full((count, model)),
            full((count, model)),
            full((1, model)),
        ],
        [((count, model), F32), vec, vec],
        [full((count, model)), *[full((1, model))] * 2],
        (steps,),
        scratch=[pltpu.VMEM((count, model), F32)],
        after=after,
        flops=2 * count * model * model * parts,
    )


def layer_result(hidden, w_down, middle, down_bias, after=()):
    count, ff = hidden.shape
    model = w_down.shape[1]
    steps = ff // TILE

    def body(h, w, mid, b, out, total):
        j = pl.program_id(0)

        @pl.when(j == 0)
        def _():
            total[...] = mid[...] + b[...] + dot(h[...], w[...])

        @pl.when(j > 0)
        def _():
            total[...] += dot(h[...], w[...])

        @pl.when(j == steps - 1)
        def _():
            out[...] = total[...].astype(BF)

    return kernel_call(
        body,
        (hidden, w_down, middle, down_bias),
        [
            pl.BlockSpec((count, TILE), lambda j: (0, j)),
            pl.BlockSpec((TILE, model), lambda j: (j, 0)),
            full((count, model)),
            full((1, model)),
        ],
        [((count, model), BF)],
        [full((count, model))],
        (steps,),
        scratch=[pltpu.VMEM((count, model), F32)],
        after=after,
        flops=2 * count * model * ff,
    )[0]


def swap(v, pairs):
    return lax.ppermute(v, AXES, pairs)


def states_before(own, doc_end, n_rows, n_seq, later=False):
    me = lax.axis_index("seq")

    def reaches(a, b):
        def at(i):
            return lax.dynamic_index_in_dim(doc_end, i, 1, keepdims=False)

        return (at(a) == at(b)).astype(F32)[:, None, None, None]

    total = own.astype(F32)
    found = jnp.zeros_like(total)
    size = 1
    while size < n_seq:
        pairs = [(r * n_seq + s, r * n_seq + (s ^ size)) for r in range(n_rows) for s in range(n_seq)]
        if 2 * size == n_seq:
            pairs = [p for p in pairs if bool(p[0] % n_seq & size) == later]
        got = swap(total.astype(BF), pairs).astype(F32)
        bit = (me // size) % 2
        group = me // (2 * size) * (2 * size)
        low, mid, high = group, group + size, group + 2 * size
        if later:
            found = found + jnp.where(bit == 0, reaches(me + 1, mid) * got, 0.0)
            same = reaches(low, mid)
            total = jnp.where(bit == 0, total + same * got, got + same * total)
        else:
            found = found + jnp.where(bit == 1, reaches(mid, me) * got, 0.0)
            same = reaches(mid, high)
            total = jnp.where(bit == 0, got + same * total, total + same * got)
        size *= 2
    return found


def stage_pairs(n_rows, n_seq):
    def pairs(bit0, bit1):
        return [(i, i ^ (bit1 if i & 1 else bit0)) for i in range(n_rows * n_seq)]

    return [pairs(2, 4), pairs(8, 8), pairs(4, 2), pairs(16, 16)]


def core_pairs(n):
    return [(i, i ^ 1) for i in range(n)]


def shard_order(device):
    j = jnp.arange(32, dtype=jnp.int32)
    core = device & 1
    first, second = jnp.where(core == 0, 1, 2), jnp.where(core == 0, 2, 1)
    flip = 31 - j
    bit = lambda k: (flip >> k) & 1
    move = bit(4) << first | bit(3) << 3 | bit(2) << second | bit(1) << 4 | bit(0)
    return device ^ move


def halvings(send, keep, stages):
    for k, pairs in enumerate(stages):
        total = keep.astype(F32) + swap(send, pairs).astype(F32)
        if k == len(stages) - 1:
            return total
        half = total.shape[0] // 2
        send, keep = total[:half].astype(BF), total[half:]


def cores_join(total, core, n):
    half = total.shape[0] // 2
    got = swap(total[:half].astype(BF), core_pairs(n)).astype(F32)
    mine = total[half:]
    return jnp.where(core == 0, mine, got), jnp.where(core == 0, got, mine)


def local(
    tokens, bounds, norm1_gain, norm1_bias, w_qkv, w_proj, norm2_gain, norm2_bias,
    w_up, up_bias, w_down, down_bias, cotangent, n_rows, n_seq,
):
    rows, span, model = tokens.shape
    ff = w_up.shape[1]
    count, n = rows * span, n_rows * n_seq
    seq = lax.axis_index("seq")
    device = lax.axis_index("rows") * n_seq + seq
    core = device & 1
    lb = bounds - seq * span
    ends = jnp.arange(n_seq + 1, dtype=jnp.int32) * span - 1
    doc_end = jnp.sum((bounds[:, None, :] <= ends[None, :, None]).astype(jnp.int32), -1)
    x, cot = tokens.reshape(count, model), cotangent.reshape(count, model)
    vec = lambda v: v.reshape(1, -1)
    gain1, bias1, gain2, bias2 = map(vec, (norm1_gain, norm1_bias, norm2_gain, norm2_bias))

    n1, km, v, own = keys_values(lb, x, gain1, bias1, w_qkv, span)
    state = states_before(own, doc_end, n_rows, n_seq)
    qm = queries(n1, w_qkv, after=(own,))
    d_act = active_grads(cot, w_down, after=(qm,))
    numer, denom = attend_inside(lb, qm, km, v, span, after=(d_act,))
    att, rden, middle, n2 = attend_join(lb, state, qm, numer, denom, x, w_proj, gain2, bias2, span)
    hidden, hidden_t, d_pre, g_up_bias = expand(n2, w_up, vec(up_bias), d_act)

    shards = 32
    fast = n == shards and model % (shards * 32) == 0 and ff % (shards * 128) == 0
    if fast:
        stages = stage_pairs(n_rows, n_seq)
        order = shard_order(device)
        place = jnp.zeros((shards,), jnp.int32).at[order].set(jnp.arange(shards, dtype=jnp.int32))
        own_table = jnp.concatenate([order, core[None]])
        other_table = jnp.concatenate([shard_order(device ^ 1), 1 - core[None]])

        def grad_pair(lhs_t, rhs, first, steps, side, after=()):
            per = rhs.shape[-1] // TILE

            def block_of(j, t):
                at = t[shards] * side + first + j
                return (0, at) if rhs.ndim == 2 else (at // per, 0, lax.rem(at, per))

            other = weight_grad(lhs_t, rhs, block_of, steps, other_table, after=after)
            got = swap(other, core_pairs(n))
            return lambda after=(): weight_grad(lhs_t, rhs, block_of, steps, own_table, got, after=after)

        def down_pair(k, per_side, after=()):
            width = model // 2 // per_side
            column = lambda t: t[shards] * per_side + k
            other = down_grad(hidden_t, cot, width, column, other_table, after=after)
            got = swap(other, core_pairs(n))
            return lambda after=(): down_grad(hidden_t, cot, width, column, own_table, got, after=after)

        down1 = down_pair(0, 2)
        down2 = down_pair(1, 2)
        s_d1 = down1()
        s_d2 = down2()
        n2_t = turned(n2, place, shards)
        up1 = grad_pair(n2_t, d_pre, 0, 2, 4)
        up2 = grad_pair(n2_t, d_pre, 2, 2, 4)
        s_u1 = up1()
        s_u2 = up2()
    d_mid, branch, g_gain2, g_bias2, g_down_bias = second_norm_grads(d_pre, w_up, middle, cot, gain2)
    d_num, d_den, d_state = mixer_grads(lb, branch, w_proj, att, rden, qm, span)
    d_own = states_before(d_state, doc_end, n_rows, n_seq, later=True)
    if fast:
        att_t = turned(att, place, shards)
        s_p = grad_pair(att_t, branch, 0, 1, 1)()
        n1_t = turned(n1, place, shards)
    layer_out = layer_result(hidden, w_down, middle, vec(down_bias))
    d_mixed = attend_back(lb, qm, km, v, d_num, d_den, state, d_own, span)
    if fast:
        q1 = grad_pair(n1_t, d_mixed, 0, 2, 3)
        q2 = grad_pair(n1_t, d_mixed, 2, 1, 3)
        s_q1 = q1()
        s_q2 = q2()
    grad_tokens, g_gain1, g_bias1 = first_norm_grads(d_mixed, w_qkv, x, d_mid, gain1)
    small = [g_gain1, g_bias1, g_gain2, g_bias2, g_up_bias, g_down_bias]
    if fast:
        done = [cores_join(halvings(*s, stages), core, n) for s in (s_d1, s_d2, s_u1, s_u2, s_p, s_q1, s_q2)]
        join = lambda *pairs: jnp.concatenate([p[0] for p in pairs] + [p[1] for p in pairs], 1)
        g_down, g_up = join(*done[0:2]), join(*done[2:4])
        g_proj, g_qkv = join(done[4]), join(*done[5:7])
        packed = jnp.concatenate([s.reshape(shards, -1) for s in small], 1)
        packed = jnp.take(packed, order, axis=0).reshape(shards // 2, 2, -1)
        sent = packed[:, 0].reshape(2, 2, 2, 2, -1).transpose(2, 1, 0, 3, 4).reshape(shards // 2, -1)
        total = packed[:, 1] + swap(sent, core_pairs(n))
        for pairs in stages:
            half = total.shape[0] // 2
            total = total[half:] + swap(total[:half], pairs)
        cuts, at = [], 0
        for s in small:
            cuts.append(total[0, at : at + s.shape[1] // shards])
            at += s.shape[1] // shards
        small = cuts
    else:
        scatter = lambda g: lax.psum_scatter(g, AXES, scatter_dimension=0, tiled=True)
        flat = d_mixed.transpose(1, 0, 2).reshape(count, 3 * model)
        g_qkv, g_proj, g_up = (scatter(dot_tn(a, b)) for a, b in ((n1, flat), (att, branch), (n2, d_pre)))
        g_down = scatter(dot_tn(hidden, cot))
        small = [scatter(s.reshape(-1)) for s in small]
    shape = (rows, span, model)
    return (
        layer_out.reshape(shape), grad_tokens.reshape(shape), small[0], small[1], g_qkv, g_proj,
        small[2], small[3], g_up, small[4], g_down, small[5],
    )


def solution(mesh):
    wide, row, whole = P("rows", "seq", None), P(AXES), P()
    in_specs = (wide, P("rows", None), *[whole] * 10, wide)
    out_specs = (wide, wide, *[row] * 10)
    body = functools.partial(local, n_rows=mesh.shape["rows"], n_seq=mesh.shape["seq"])
    return jax.shard_map(body, mesh=mesh, in_specs=in_specs, out_specs=out_specs, check_vma=False)
```

```python
import functools

import jax
import jax.numpy as jnp
from jax import lax
from jax.experimental import pallas as pl
from jax.experimental.pallas import tpu as pltpu
from jax.sharding import PartitionSpec as P

HEADS = 16
EPS = 1e-05
BF, F32 = jnp.bfloat16, jnp.float32
AXES = ("rows", "seq")
SUMS = 64
DEPTH = 80
TILE = 512


def dot(a, b):
    return jnp.dot(a, b, preferred_element_type=F32)


def dot_nt(a, b):
    return lax.dot_general(a, b, (((1,), (1,)), ((), ())), preferred_element_type=F32)


def dot_tn(a, b):
    return lax.dot_general(a, b, (((0,), (0,)), ((), ())), preferred_element_type=F32)


def iota(shape, dim):
    return lax.broadcasted_iota(jnp.int32, shape, dim)


SMEM = pl.BlockSpec(memory_space=pltpu.SMEM)
WHOLE = pl.BlockSpec(memory_space=pltpu.VMEM)
HBM = pl.BlockSpec(memory_space=pltpu.HBM)


def cut(at, size):
    return pl.ds(pl.multiple_of(at, size), size)


def in_vmem(x):
    return pltpu.with_memory_space_constraint(x, pltpu.VMEM)


def kernel_call(body, scalars, args, outs, scratch=(), far=(), hold=(), fetch=(), time=0.5, limit=7):
    n_in, n_hold, n_fetch, n_out = len(scalars) + len(args) + len(far), len(hold), len(fetch), len(outs)
    every = [(*o, True)[:3] for o in outs]
    every += [(f.shape, f.dtype, True) for f in fetch] + [((8, 128), F32, True)]

    def wrapped(*refs):
        ins, rest = refs[:n_in], refs[n_in + n_hold :]
        sources, rest = rest[:n_fetch], rest[n_fetch:]
        results, targets = rest[:n_out], rest[n_out : n_out + n_fetch]
        token, rest = rest[n_out + n_fetch], rest[n_out + n_fetch + 1 :]
        copies = []
        if n_fetch:
            sems, rest = rest[-1], rest[:-1]
            copies = [pltpu.make_async_copy(a, b, sems.at[k]) for k, (a, b) in enumerate(zip(sources, targets))]
        for copy in copies:
            copy.start()
        token[...] = jnp.zeros_like(token)
        body(*ins, *results, *rest)
        for copy in copies:
            copy.wait()

    shapes = [pltpu.VMEM(s, d) if v else jax.ShapeDtypeStruct(s, d) for s, d, v in every]
    in_hbm = lambda x: pltpu.with_memory_space_constraint(x, pltpu.HBM)
    out = pl.pallas_call(
        wrapped,
        in_specs=[SMEM] * len(scalars)
        + [WHOLE] * len(args)
        + [HBM] * len(far)
        + [WHOLE] * n_hold
        + [HBM] * n_fetch,
        out_specs=[WHOLE] * len(every),
        out_shape=shapes,
        scratch_shapes=[*scratch, *([pltpu.SemaphoreType.DMA((n_fetch,))] if n_fetch else [])],
        compiler_params=pltpu.CompilerParams(vmem_limit_bytes=limit << 20),
        cost_estimate=pl.CostEstimate(flops=int(time * 1e10), bytes_accessed=1, transcendentals=0),
    )(*scalars, *map(in_vmem, args), *map(in_hbm, far), *map(in_vmem, hold), *map(in_hbm, fetch))
    return out


def normal(x):
    center = x - jnp.mean(x, -1, keepdims=True)
    root = lax.rsqrt(jnp.mean(center * center, -1, keepdims=True) + EPS)
    return center * root, root


def feature(u):
    return jnp.where(u > 0, u + 1.0, jnp.exp(jnp.minimum(u, 0.0)))


def keep_from(lb, row, span):
    last = 0 - span
    for k in range(lb.shape[1]):
        last = jnp.where(lb[row, k] < span, jnp.maximum(last, lb[row, k]), last)
    return last


def carry_to(lb, row, span):
    end = span
    for k in range(lb.shape[1]):
        end = jnp.where(lb[row, k] >= 0, jnp.minimum(end, lb[row, k]), end)
    return end


def block_mask(lb, row, span):
    t, s = iota((span, span), 0), iota((span, span), 1)
    ok = s <= t
    for k in range(lb.shape[1]):
        ok = ok & ((lb[row, k] > t) | (s >= lb[row, k]))
    return ok.astype(F32)


def pack_state(m):
    half = m.shape[0] // 2
    return jnp.where(iota((half, m.shape[1]), 1) < half, m[:half], m[half:])


def unpack_state(c):
    half = c.shape[0]
    left = iota(c.shape, 1) < half
    return jnp.concatenate([jnp.where(left, c, 0.0), jnp.where(left, 0.0, c)], 0)


def split(x):
    hi = x.astype(BF)
    return hi, (x - hi.astype(F32)).astype(BF)


def head_ones(lanes=128):
    half = lanes // 2
    return ((iota((lanes, lanes), 0) < half) == (iota((lanes, lanes), 1) < half)).astype(BF)


def head_sum(x):
    hi, lo = split(x)
    ones = head_ones(x.shape[1])
    return dot(jnp.concatenate([hi, lo], 1), jnp.concatenate([ones, ones], 0))


def dot_split(a, m):
    hi, lo = split(m)
    return dot(jnp.concatenate([a, a], 1), jnp.concatenate([hi, lo], 0))


def keys_values(lb, tokens, vectors, w_qkv, span, **kw):
    count, model = tokens.shape
    rows, width = count // span, 256
    n_vec, blocks = len(vectors), model // 512

    def body(lb, *refs):
        x_in, vec_in, w_in = refs[0], refs[1 : 1 + n_vec], refs[1 + n_vec]
        n1, km, v, own, *vecs = refs[2 + n_vec : 6 + 2 * n_vec]
        x, w, sems = refs[6 + 2 * n_vec :]

        def copy(k, a, b):
            return pltpu.make_async_copy(a, b, sems.at[k])

        def columns(j):
            lanes = slice(j * 512, (j + 1) * 512)
            return copy(1 + n_vec + j, w_in.at[:, model + j * 512 : model + (j + 1) * 512], w.at[:, lanes])

        head = [copy(0, x_in, x)] + [copy(1 + k, a, b) for k, (a, b) in enumerate(zip(vec_in, vecs))]
        for c in head:
            c.start()
        for c in [c for j in range(blocks) for c in (j, blocks + j)]:
            columns(c).start()
        for c in head:
            c.wait()

        @pl.loop(0, count // 64, unroll=2)
        def _(i):
            at = cut(i * 64, 64)
            n1[at] = (normal(x[at].astype(F32))[0] * vecs[0][...] + vecs[1][...]).astype(BF)

        kept = [iota((span, width), 0) >= keep_from(lb, r, span) for r in range(rows)]
        for j in range(model // width):
            if j * width % 512 == 0:
                columns(j * width // 512).wait()
                columns(blocks + j * width // 512).wait()
            lanes = slice(j * width, (j + 1) * width)
            key = feature(dot(n1[...], w[:, lanes])).astype(BF)
            val = dot(n1[...], w[:, model + j * width : model + (j + 1) * width]).astype(BF)
            km[:, lanes], v[:, lanes] = key, val
            for r in range(rows):
                part = slice(r * span, (r + 1) * span)
                owned = jnp.where(kept[r], key[part], jnp.zeros((), BF))
                for p in range(width // 128):
                    at = slice(p * 128, (p + 1) * 128)
                    block = j * (width // 128) + p
                    own[r, block, 0:SUMS] = pack_state(dot_tn(owned[:, at], val[part, at])).astype(BF)
                    total = jnp.sum(owned[:, at].astype(F32), 0, keepdims=True)
                    own[r, block, SUMS:DEPTH] = jnp.broadcast_to(total, (DEPTH - SUMS, 128)).astype(BF)

    wide = ((count, model), BF)
    outs = [wide, wide, wide, ((rows, model // 128, DEPTH, 128), BF)]
    outs += [(v.shape, v.dtype) for v in vectors]
    return kernel_call(
        body, (lb,), (), outs, far=(tokens, *vectors, w_qkv),
        scratch=[
            pltpu.VMEM((count, model), BF),
            pltpu.VMEM((model, 2 * model), BF),
            pltpu.SemaphoreType.DMA((1 + n_vec + 2 * blocks,)),
        ],
        limit=9, time=7.3, **kw,
    )


def merge_states(coefs, own, got, **kw):
    rows = own.shape[0]

    def body(c, a, b, out):
        for r in range(rows):
            out[r] = (c[0, r] * a[r].astype(F32) + c[1, r] * b[r].astype(F32)).astype(BF)

    return kernel_call(body, (coefs,), (own, got), [(own.shape, BF)], **kw)


def queries(normed, w_qkv, **kw):
    count, model = normed.shape
    tiles = model // 256

    def body(n, w_in, q, w, sems):
        copies = [
            pltpu.make_async_copy(w_in.at[:, j * 256 : (j + 1) * 256], w.at[:, j * 256 : (j + 1) * 256], sems.at[j])
            for j in range(tiles)
        ]
        for c in copies:
            c.start()
        for j in range(tiles):
            lanes = slice(j * 256, (j + 1) * 256)
            copies[j].wait()
            q[:, lanes] = feature(dot(n[...], w[:, lanes])).astype(BF)

    return kernel_call(
        body, (), (normed,), [((count, model), BF)], far=(w_qkv,),
        scratch=[pltpu.VMEM((model, model), BF), pltpu.SemaphoreType.DMA((tiles,))],
        limit=5, time=3.9, **kw,
    )


def active_grads(cotangent, w_down, **kw):
    count, model = cotangent.shape
    ff = w_down.shape[0]

    def body(c, w, out):
        for j in range(ff // TILE):
            lanes = slice(j * TILE, (j + 1) * TILE)
            out[:, lanes] = dot_nt(c[...], w[lanes, :])

    return kernel_call(
        body, (), (cotangent, w_down), [((count, ff), F32)], time=4.5, **kw
    )


def attend_inside(lb, query, key, values, span, **kw):
    count, model = query.shape
    rows = count // span

    def body(lb, q_ref, k_ref, v_ref, numer, denom, mask):
        for r in range(rows):
            mask[r] = block_mask(lb, r, span)
        left = iota((span, 128), 1) < 64
        zero = jnp.zeros((), BF)

        @pl.loop(0, model // 128)
        def _(p):
            lanes = cut(p * 128, 128)
            for r in range(rows):
                part = slice(r * span, (r + 1) * span)
                q, k, v = q_ref[part, lanes], k_ref[part, lanes], v_ref[part, lanes]
                total = 0.0
                for e in range(2):
                    mine = left if e == 0 else ~left
                    scores = dot_nt(jnp.where(mine, q, zero), k)
                    weights = (scores * mask[r]).astype(BF)
                    both = jnp.concatenate([jnp.where(mine, v, zero), mine.astype(BF)], 1)
                    total = total + dot(weights, both)
                numer[part, lanes] = total[:, :128]
                denom[part, lanes] = total[:, 128:]

    wide = ((count, model), F32)
    return kernel_call(
        body, (lb,), (query, key, values), [wide, wide],
        scratch=[pltpu.VMEM((rows, span, span), F32)], time=5.7, **kw,
    )


def state_of(coefs, gots, r, p):
    total = 0.0
    for i, got in enumerate(gots):
        total = total + coefs[i, r] * got[r, p].astype(F32)
    return total


def attend_join(lb, coefs, gots, query, numer, denom, tokens, w_proj, gain, bias, span, **kw):
    count, model = query.shape
    pairs, n = model // 128, len(gots)
    rows = count // span

    def body(lb, coefs, *refs):
        gots, (q_ref, num_ref, den_ref, x, w, g, b, att, rden, middle, n2) = refs[:n], refs[n:]
        place = iota((span, 128), 0)

        @pl.loop(0, pairs)
        def _(p):
            lanes = cut(p * 128, 128)
            for r in range(rows):
                part = slice(r * span, (r + 1) * span)
                state = state_of(coefs, gots, r, p)
                q = jnp.where(place < carry_to(lb, r, span), q_ref[part, lanes], jnp.zeros((), BF))
                num = num_ref[part, lanes] + dot_split(q, unpack_state(state[0:SUMS]))
                den = den_ref[part, lanes] + head_sum(q.astype(F32) * state[SUMS : SUMS + 1])
                inv = 1.0 / den
                rden[part, lanes] = inv
                att[part, lanes] = (num * inv).astype(BF)

        for j in range(model // 256):
            lanes = slice(j * 256, (j + 1) * 256)
            middle[:, lanes] = x[:, lanes].astype(F32) + dot(att[...], w[:, lanes])

        @pl.loop(0, count // 64, unroll=2)
        def _(i):
            at = cut(i * 64, 64)
            n2[at] = (normal(middle[at])[0] * g[...] + b[...]).astype(BF)

    wide = (count, model)
    return kernel_call(
        body, (lb, coefs), (*gots, query, numer, denom, tokens, w_proj, gain, bias),
        [(wide, BF), (wide, F32), (wide, F32), (wide, BF)],
        time=5.0, **kw,
    )


def expand(normed, w_up, up_bias, d_active, **kw):
    count, model = normed.shape
    ff = w_up.shape[1]
    c0, c1 = 0.7978845608028654, 0.7978845608028654 * 0.044715
    step = 32

    def body(n, w, b, da, hid, dp, total, even, odd):
        quarter = count // 4
        ones = jnp.ones((16, count), BF)

        def rest(j, u_ref, k):
            lanes = cut(j * TILE, TILE)
            bias = b[:, lanes]
            for i in range(k * quarter // step, (k + 1) * quarter // step):
                at = slice(i * step, (i + 1) * step)
                u = u_ref[at] + bias
                sq = u * u
                t = jnp.tanh(u * (c0 + c1 * sq))
                half = 0.5 * u
                rise = 1.0 + t
                hid[at, lanes] = (half * rise).astype(BF)
                slope = rise * (0.5 + half * (1.0 - t) * (c0 + 3.0 * c1 * sq))
                dp[at, lanes] = (slope * da[at, lanes]).astype(BF)

        def tile(j, out, j_last, last):
            for k in range(4):
                if j is not None:
                    at = slice(k * quarter, (k + 1) * quarter)
                    out[at] = dot(n[at], w[:, cut(j * TILE, TILE)])
                if last is not None:
                    rest(j_last, last, k)
            if last is not None:
                lanes = cut(j_last * TILE, TILE)
                total[:, lanes] = dot(ones, dp[:, lanes])[0:1]

        tiles = ff // TILE
        tile(0, even, None, None)

        @pl.loop(0, tiles // 2 - 1)
        def _(i):
            tile(2 * i + 1, odd, 2 * i, even)
            tile(2 * i + 2, even, 2 * i + 1, odd)

        tile(tiles - 1, odd, tiles - 2, even)
        tile(None, None, tiles - 1, odd)

    wide = ((count, ff), BF)
    return kernel_call(
        body, (), (normed, w_up, up_bias, d_active), [wide, wide, ((1, ff), F32)],
        scratch=[pltpu.VMEM((count, TILE), F32)] * 2, limit=6, time=11.0, **kw,
    )


def turned(x, tables, shards, **kw):
    count, model = x.shape
    deep = model // shards

    def body(tables, x, out):
        for j in range(model // 128):
            t = x[:, j * 128 : (j + 1) * 128].T
            for k in range(128 // deep):
                out[cut(tables[2, j * (128 // deep) + k] * deep, deep), :] = t[k * deep : (k + 1) * deep]

    return kernel_call(body, (tables,), (x,), [((model, count), BF)], **kw)


def weight_grad(lhs_t, rhs, first, steps, side, tables, got=None, **kw):
    deep, count = lhs_t.shape
    shards = tables.shape[1]
    rows, half = deep // shards, deep // 2
    time = 0.9 * steps
    shape = (deep, TILE * steps)

    def tile(b, which, j):
        return b[:, cut((which * side + first + j) * TILE, TILE)]

    if got is None:

        def body(tables, a, b, out):
            for j in range(steps):
                total = dot(a[...], tile(b, 1 - tables[3, 0], j)).astype(BF)
                for k in range(shards):
                    at = (k & 0b01010) | (k >> 4 & 1) << 2 | (k >> 2 & 1) << 4 | (~k & 1)
                    out[at * rows : (at + 1) * rows, j * TILE : (j + 1) * TILE] = total[k * rows : (k + 1) * rows]

        return kernel_call(body, (tables,), (lhs_t, rhs), [(shape, BF)], time=time, **kw)

    def body(tables, a, b, g, send, keep):
        for j in range(steps):
            lanes = slice(j * TILE, (j + 1) * TILE)
            total = dot(a[...], tile(b, tables[3, 0], j)) + g[:, lanes].astype(F32)
            send[:, lanes] = total[:half].astype(BF)
            keep[:, lanes] = total[half:].astype(BF)

    return kernel_call(
        body, (tables,), (lhs_t, rhs, got), [((half, TILE * steps), BF)] * 2, time=time, **kw
    )


def down_grad(hidden, cotangent, width, first, side, tables, got=None, **kw):
    count, ff = hidden.shape
    shards = tables.shape[1]
    deep = ff // shards
    per = TILE // deep
    steps = ff // TILE
    time = width / 110

    def product(tables, h, c, i, mine):
        which = 0 if mine else 1
        core = tables[3, 0]
        column = pl.multiple_of((core if mine else 1 - core) * side + first, 128)
        lhs = [h[:, cut(tables[which, per * i + k] * deep, deep)] for k in range(per)]
        return dot_tn(jnp.concatenate(lhs, 1), c[:, pl.ds(column, width)])

    if got is None:

        def body(tables, h, c, out):
            for i in range(steps):
                out[i * TILE : (i + 1) * TILE] = product(tables, h, c, i, False).astype(BF)

        return kernel_call(body, (tables,), (hidden, cotangent), [((ff, width), BF)], time=time, **kw)

    def body(tables, h, c, g, send, keep):
        for i in range(steps):
            total = product(tables, h, c, i, True) + g[i * TILE : (i + 1) * TILE].astype(F32)
            out, at = (send, i) if i < steps // 2 else (keep, i - steps // 2)
            out[at * TILE : (at + 1) * TILE] = total.astype(BF)

    return kernel_call(
        body, (tables,), (hidden, cotangent, got), [((ff // 2, width), BF)] * 2, time=time, **kw
    )


def norm_grad_rows(e_ref, x_of, gain, count, write):
    step, model = 32, gain.shape[1]

    def one(i, sums):
        at = cut(i * step, step)
        e = e_ref[at]
        hat, root = normal(x_of(at))
        g = e * gain[...]
        back = root * (g - jnp.mean(g, -1, keepdims=True) - hat * jnp.mean(g * hat, -1, keepdims=True))
        write(at, back)
        eights = lambda v: jnp.sum(v.reshape(step // 8, 8, model), 0)
        return sums[0] + eights(e * hat), sums[1] + eights(e)

    zero = jnp.zeros((8, model), F32)
    sums = lax.fori_loop(0, count // step, one, (zero, zero), unroll=4)
    return [jnp.sum(s, 0, keepdims=True) for s in sums]


def second_norm_grads(d_pre, w_up, middle, cotangent, gain, **kw):
    count, ff = d_pre.shape
    model = w_up.shape[0]

    def body(d, w, mid, cot, g, d_mid, branch, g_gain, g_bias, g_down, e):
        for j in range(model // 256):
            lanes = slice(j * 256, (j + 1) * 256)
            e[:, lanes] = dot_nt(d[...], w[lanes, :])

        def write(at, back):
            out = cot[at].astype(F32) + back
            d_mid[at] = out
            branch[at] = out.astype(BF)

        g_gain[...], g_bias[...] = norm_grad_rows(e, lambda at: mid[at], g, count, write)
        g_down[...] = jnp.sum(cot[...].astype(F32), 0, keepdims=True)

    vec, wide = ((1, model), F32), (count, model)
    return kernel_call(
        body, (), (d_pre, w_up, middle, cotangent, gain), [(wide, F32), (wide, BF), vec, vec, vec],
        scratch=[pltpu.VMEM(wide, F32)], time=7.0, **kw,
    )


def mixer_grads(lb, branch, w_proj, attended, rden, query, span, **kw):
    count, model = branch.shape
    rows, pairs = count // span, model // 128

    def body(lb, br, w, att, rd, q_ref, dn, dd, own):
        place = iota((span, 128), 0)
        for j in range(model // 256):
            d_att = dot_nt(br[...], w[j * 256 : (j + 1) * 256, :])
            for k in range(2):
                p = 2 * j + k
                lanes = slice(p * 128, (p + 1) * 128)
                for r in range(rows):
                    part = slice(r * span, (r + 1) * span)
                    d, inv = d_att[part, k * 128 : (k + 1) * 128], rd[part, lanes]
                    d_den = -head_sum(d * att[part, lanes].astype(F32)) * inv
                    d_num = (d * inv).astype(BF)
                    dn[part, lanes], dd[part, lanes] = d_num, d_den
                    q = jnp.where(place < carry_to(lb, r, span), q_ref[part, lanes], jnp.zeros((), BF))
                    own[r, p, 0:SUMS] = pack_state(dot_tn(q, d_num)).astype(BF)
                    total = jnp.sum(d_den * q.astype(F32), 0, keepdims=True)
                    own[r, p, SUMS:DEPTH] = jnp.broadcast_to(total, (DEPTH - SUMS, 128)).astype(BF)

    wide = (count, model)
    return kernel_call(
        body, (lb,), (branch, w_proj, attended, rden, query),
        [(wide, BF), (wide, F32), ((rows, pairs, DEPTH, 128), BF)],
        time=5.0, **kw,
    )


def attend_back(lb, coefs, back_coefs, gots, back_gots, query, key, values, d_num, d_den, span, **kw):
    count, model = query.shape
    rows, n, m = count // span, len(gots), len(back_gots)

    def body(lb, coefs, back_coefs, *refs):
        gots, back_gots = refs[:n], refs[n : n + m]
        q_ref, k_ref, v_ref, dn_ref, dd_ref, out, mask, mask_t = refs[n + m :]
        for r in range(rows):
            ok = block_mask(lb, r, span)
            mask[r], mask_t[r] = ok, ok.T
        lane, place = iota((span, 128), 1), iota((span, 128), 0)
        left = lane < 64
        zero = jnp.zeros((), BF)

        @pl.loop(0, model // 128)
        def _(p):
            lanes = cut(p * 128, 128)
            for r in range(rows):
                part = slice(r * span, (r + 1) * span)
                carried = place < carry_to(lb, r, span)
                kept = place >= keep_from(lb, r, span)
                q, k, v = q_ref[part, lanes], k_ref[part, lanes], v_ref[part, lanes]
                dn, dd = dn_ref[part, lanes], dd_ref[part, lanes]
                hi, lo = split(dd)
                v_ones = jnp.concatenate([v, jnp.ones_like(v)], 1)
                dq = dk = dv = 0.0
                for e in range(2):
                    mine = left if e == 0 else ~left
                    at = 64 * e
                    qm, dnm = jnp.where(mine, q, zero), jnp.where(mine, dn, zero)
                    extra = jnp.where(lane == at, hi, jnp.where(lane == at + 1, lo, zero))
                    dn_den = jnp.concatenate([dnm, extra], 1)
                    ds = (dot_nt(dn_den, v_ones) * mask[r]).astype(BF)
                    ds_t = (dot_nt(v_ones, dn_den) * mask_t[r]).astype(BF)
                    w_t = (dot_nt(k, qm) * mask_t[r]).astype(BF)
                    dq = dq + dot(ds, jnp.where(mine, k, zero))
                    dk = dk + dot(ds_t, qm)
                    dv = dv + dot(w_t, dnm)
                state, own = state_of(coefs, gots, r, p), state_of(back_coefs, back_gots, r, p)
                s_hi, s_lo = split(unpack_state(state[0:SUMS]))
                o_hi, o_lo = split(unpack_state(own[0:SUMS]))
                through_s = dot_nt(jnp.concatenate([dn, dn], 1), jnp.concatenate([s_hi, s_lo], 1))
                through_o = dot_nt(jnp.concatenate([v, v], 1), jnp.concatenate([o_hi, o_lo], 1))
                through_k = dot(jnp.concatenate([k, k], 1), jnp.concatenate([o_hi, o_lo], 0))
                dq = dq + jnp.where(carried, through_s + dd * state[SUMS : SUMS + 1], 0.0)
                dk = dk + jnp.where(kept, through_o + own[SUMS : SUMS + 1], 0.0)
                dv = dv + jnp.where(kept, through_k, 0.0)
                out[part, lanes] = (dq * jnp.minimum(q.astype(F32), 1.0)).astype(BF)
                out[part, cut(model + p * 128, 128)] = (dk * jnp.minimum(k.astype(F32), 1.0)).astype(BF)
                out[part, cut(2 * model + p * 128, 128)] = dv.astype(BF)

    return kernel_call(
        body, (lb, coefs, back_coefs), (*gots, *back_gots, query, key, values, d_num, d_den),
        [((count, 3 * model), BF)],
        scratch=[pltpu.VMEM((rows, span, span), F32)] * 2, time=12.0, **kw,
    )


def first_norm_grads(d_mixed, w_qkv, tokens, d_middle, gain, others, **kw):
    count = d_mixed.shape[0]
    model = w_qkv.shape[0]

    n = len(others)

    def body(d, w, x, dm, g, *refs):
        rest, (out, packed, e) = refs[:n], refs[n:]
        for j in range(model // 256):
            lanes = slice(j * 256, (j + 1) * 256)
            e[:, lanes] = dot_nt(d[...], w[lanes, :])

        def write(at, back):
            out[at] = dm[at] + back

        at = 0
        for part in (*norm_grad_rows(e, lambda at: x[at].astype(F32), g, count, write), *[r[...] for r in rest]):
            packed[:, at : at + part.shape[1]] = part
            at += part.shape[1]

    wide, size = (count, model), 2 * model + sum(o.shape[1] for o in others)
    return kernel_call(
        body, (), (d_mixed, w_qkv, tokens, d_middle, gain, *others), [(wide, F32, False), ((1, size), F32)],
        scratch=[pltpu.VMEM(wide, F32)], limit=8, time=6.5, **kw,
    )


def layer_result(hidden, w_down, middle, down_bias, **kw):
    count, ff = hidden.shape
    model = w_down.shape[1]

    def body(h, w, mid, b, out):
        for j in range(model // 256):
            lanes = slice(j * 256, (j + 1) * 256)
            out[:, lanes] = (mid[:, lanes] + dot(h[...], w[:, lanes]) + b[:, lanes]).astype(BF)

    return kernel_call(
        body, (), (hidden, w_down, middle, down_bias), [((count, model), BF, False)],
        time=5.5, **kw,
    )


def swap(v, pairs):
    return lax.ppermute(v, AXES, pairs)


def state_plan(doc_end, n_rows, n_seq, later=False):
    me = lax.axis_index("seq")

    def reaches(a, b):
        def at(i):
            return lax.dynamic_index_in_dim(doc_end, i, 1, keepdims=False)

        return (at(a) == at(b)).astype(F32)

    pairs, merges, coefs = [], [], []
    size = 1
    while size < n_seq:
        step = [(r * n_seq + s, r * n_seq + (s ^ size)) for r in range(n_rows) for s in range(n_seq)]
        if 2 * size == n_seq:
            step = [p for p in step if bool(p[0] % n_seq & size) == later]
        pairs.append(step)
        upper = (me // size) % 2 == 1
        low = me // (2 * size) * (2 * size)
        mid, high = low + size, low + 2 * size
        if later:
            coefs.append(jnp.where(upper, 0.0, reaches(me + 1, mid)))
            same = reaches(low, mid)
            merges.append(jnp.stack([jnp.where(upper, same, 1.0), jnp.where(upper, 1.0, same)]))
        else:
            coefs.append(jnp.where(upper, reaches(mid, me), 0.0))
            same = reaches(mid, high)
            merges.append(jnp.stack([jnp.where(upper, 1.0, same), jnp.where(upper, same, 1.0)]))
        size *= 2
    return pairs, merges, jnp.stack(coefs)


def stage_pairs(n_rows, n_seq):
    def pairs(bit0, bit1):
        return [(i, i ^ (bit1 if i & 1 else bit0)) for i in range(n_rows * n_seq)]

    return [pairs(2, 4), pairs(8, 8), pairs(4, 2), pairs(16, 16)]


def core_pairs(n):
    return [(i, i ^ 1) for i in range(n)]


def shard_tables(device):
    j = jnp.arange(32, dtype=jnp.int32)

    def bits(device):
        core = device & 1
        return jnp.where(core == 0, 1, 2), 3, jnp.where(core == 0, 2, 1), 4, 0

    def order(device):
        move = 0
        for k, at in enumerate(bits(device)):
            move = move | (((31 - j) >> (4 - k)) & 1) << at
        return device ^ move

    place = 0
    for k, at in enumerate(bits(device)):
        place = place | (1 - (((j ^ device) >> at) & 1)) << (4 - k)
    return jnp.stack([order(device), order(device ^ 1), place, jnp.broadcast_to(device & 1, (32,))])


def fold(parts, **kw):
    rows = parts[0][0].shape[0]
    widths = [k.shape[1] for k, g in parts]
    half, step, n = rows // 2, min(32, rows // 2), len(parts)

    def body(*refs):
        send, keep = refs[2 * n :]

        @pl.loop(0, half // step, unroll=min(2, half // step))
        def _(i):
            at = 0
            top, low = cut(i * step, step), cut(half + i * step, step)
            for k, w in enumerate(widths):
                a, b = refs[2 * k], refs[2 * k + 1]
                lanes = slice(at, at + w)
                send[top, lanes] = (a[top].astype(F32) + b[top].astype(F32)).astype(BF)
                keep[top, lanes] = a[low].astype(F32) + b[low].astype(F32)
                at += w

    shape = (half, sum(widths))
    return kernel_call(body, (), [x for p in parts for x in p], [(shape, BF), (shape, F32)], **kw)


def place(tables, pieces, side, **kw):
    rows = pieces[0][0].shape[0]

    def body(tables, *refs):
        core, out = tables[3, 0], refs[-1]
        for k, (mine, got, at, w, to) in enumerate(pieces):
            out[:, pl.ds(pl.multiple_of(core * side + to, 128), w)] = refs[2 * k][:, at : at + w]
            out[:, pl.ds(pl.multiple_of((1 - core) * side + to, 128), w)] = refs[2 * k + 1][:, at : at + w].astype(F32)

    args = [x for p in pieces for x in p[:2]]
    return kernel_call(body, (tables,), args, [((rows, 2 * side), F32, False)], **kw)


def settle(a, **kw):
    def body(a, out):
        out[...] = a[...]

    return kernel_call(body, (), (a,), [(a.shape, a.dtype)], **kw)


def add(a, b, **kw):
    def body(a, b, out):
        out[...] = a[...] + b[...]

    return kernel_call(body, (), (a, b), [(a.shape, a.dtype)], **kw)


def local(
    tokens, bounds, norm1_gain, norm1_bias, w_qkv, w_proj, norm2_gain, norm2_bias,
    w_up, up_bias, w_down, down_bias, cotangent, n_rows, n_seq,
):
    rows, span, model = tokens.shape
    ff = w_up.shape[1]
    count, n = rows * span, n_rows * n_seq
    seq = lax.axis_index("seq")
    device = lax.axis_index("rows") * n_seq + seq
    core = device & 1
    lb = bounds - seq * span
    ends = jnp.arange(n_seq + 1, dtype=jnp.int32) * span - 1
    doc_end = jnp.sum((bounds[:, None, :] <= ends[None, :, None]).astype(jnp.int32), -1)
    x, cot = tokens.reshape(count, model), cotangent.reshape(count, model)
    vectors = [v.reshape(1, -1) for v in (norm1_gain, norm1_bias, norm2_gain, norm2_bias, up_bias, down_bias)]
    shards = 32
    fast = n == shards and model % (shards * 32) == 0 and ff % (shards * 128) == 0
    plan = state_plan(doc_end, n_rows, n_seq)
    back_plan = state_plan(doc_end, n_rows, n_seq, later=True)
    held, last = [], []

    def run(kernel, *args, **kw):
        used = {id(x) for x in jax.tree.leaves(args)}
        small = kernel in (fold, settle, add, merge_states, turned)
        *outs, token = kernel(*args, hold=[x for x in held if id(x) not in used and not small] + last, **kw)
        last[:] = [token]
        return outs[0] if len(outs) == 1 else outs

    def keep(*arrays):
        held.extend(arrays)

    def drop(*arrays):
        held[:] = [x for x in held if all(x is not y for y in arrays)]

    def merged(plan, gots, own):
        return run(merge_states, plan[1][len(gots) - 1], own, gots[-1])

    n1, km, v, own, *vectors = run(keys_values, lb, x, vectors, w_qkv, span)
    gain1, bias1, gain2, bias2, b_up, b_down = vectors
    keep(km, v, gain1, gain2, bias2, b_up, b_down)
    gots = [swap(own, plan[0][0])]
    qm = run(queries, n1, w_qkv)
    keep(qm)
    group = own
    for pairs in plan[0][1:]:
        group = merged(plan, gots, group)
        gots.append(swap(group, pairs))
    numer, denom, wdown_v, wproj_v, cot_v = run(attend_inside, lb, qm, km, v, span, fetch=(w_down, w_proj, cot))
    drop(km, v, qm)
    keep(numer, denom, wproj_v, cot_v)
    d_act = run(active_grads, cot_v, wdown_v)
    keep(d_act)
    att, rden, middle, n2, wup_v = run(
        attend_join, lb, plan[2], gots, qm, numer, denom, x, wproj_v, gain2, bias2, span, fetch=(w_up,)
    )
    drop(numer, denom, wproj_v)
    keep(wup_v, n2)
    hidden, d_pre, g_up_bias = run(expand, n2, wup_v, b_up, d_act)
    drop(d_act)
    keep(hidden, d_pre)

    tables = shard_tables(device)
    stages = [*stage_pairs(n_rows, n_seq), core_pairs(n)] if fast else []
    state = {}

    def other(name, kernel, *args):
        if fast:
            out = run(kernel, *args, tables)
            state[name] = (kernel, args, swap(out, core_pairs(n)))

    def mine(name):
        if fast:
            kernel, args, got = state[name]
            send, kept = run(kernel, *args, tables, got)
            state[name] = (kept, swap(send, stages[0]), 1)

    def step(name, *names):
        if fast:
            parts = [state[k] for k in names or (name,)]
            send, kept = run(fold, [p[:2] for p in parts])
            at = parts[0][2]
            state[name] = (kept, swap(send, stages[at]), at + 1)

    def end(to, side, *pieces):
        if fast:
            found = []
            for name, w, column, at in pieces:
                kept, got, unused = state[name]
                found.append((kept, got, at, w, column))
            grads[to] = run(place, tables, found, side)

    def arrived(name):
        if fast:
            kept, got, at = state[name]
            state[name] = (kept, run(settle, got), at)

    grads, small_step = {}, [0]

    def small_sum():
        if fast:
            k = small_step[0]
            if k:
                state["small"] = run(add, state["small"], state["small got"])
            if k < 5:
                pairs = [(i, i ^ (1 << k)) for i in range(n)]
                state["small got"] = swap(state["small"], pairs)
            small_step[0] += 1

    half, first_piece, piece = ff // TILE // 2, 128, model // 2 - 128
    other("d1", down_grad, hidden, cot_v, first_piece, 0, model // 2)
    other("d2", down_grad, hidden, cot_v, piece, first_piece, model // 2)
    mine("d1")
    if fast:
        n2_t = run(turned, n2, tables, shards)
        drop(n2)
        other("u1", weight_grad, n2_t, d_pre, 0, half, half)
        n1_t = run(turned, n1, tables, shards)
    mine("d2")
    step("d1")
    d_mid, branch, g_gain2, g_bias2, g_down_bias, wproj_v = run(
        second_norm_grads, d_pre, wup_v, middle, cot_v, gain2, fetch=(w_proj,)
    )
    drop(wup_v, gain2, bias2, b_up, cot_v)
    keep(branch, wproj_v)
    d_num, d_den, d_state = run(mixer_grads, lb, branch, wproj_v, att, rden, qm, span)
    drop(wproj_v)
    back_gots, group = [swap(d_state, back_plan[0][0])], d_state
    step("d1")
    for pairs in back_plan[0][1:]:
        group = merged(back_plan, back_gots, group)
        back_gots.append(swap(group, pairs))
    mine("u1")
    drop(d_pre)
    step("d2")
    step("d1")
    if fast:
        att_t, wdown_v = run(turned, att, tables, shards, fetch=(w_down,))
        other("p", weight_grad, att_t, branch, 0, 1, 1)
    else:
        wdown_v = w_down
    layer_out = run(layer_result, hidden, wdown_v, middle, b_down)
    drop(hidden, b_down)
    mine("p")
    drop(branch)
    d_mixed, wqkv_v = run(
        attend_back, lb, plan[2], back_plan[2], gots, back_gots, qm, km, v, d_num, d_den, span, fetch=(w_qkv,)
    )
    keep(d_mixed, wqkv_v)
    if fast:
        other("q1", weight_grad, n1_t, d_mixed, 0, 2, 3)
    step("p")
    step("d1")
    step("d2")
    arrived("d1")
    step("u1")
    mine("q1")
    step("p")
    step("d2")
    if fast:
        other("q2", weight_grad, n1_t, d_mixed, 2, 1, 3)
    others = [g_gain2, g_bias2, g_up_bias, g_down_bias]
    grad_tokens, small = run(first_norm_grads, d_mixed, wqkv_v, x, d_mid, gain1, others)
    state["small"] = small
    drop(wqkv_v, gain1)
    mine("q2")
    drop(d_mixed)
    step("p")
    step("d2")
    step("q1")
    end("down", model // 2, ("d1", first_piece, 0, 0), ("d2", piece, first_piece, 0))
    small_sum()
    step("u1")
    step("p")
    small_sum()
    step("q2")
    end("proj", model // 2, ("p", TILE, 0, 0))
    small_sum()
    step("u1")
    small_sum()
    step("q1")
    small_sum()
    step("q2")
    small_sum()
    step("q1")
    step("q2")
    step("u1")
    end("up", ff // 2, ("u1", ff // 2, 0, 0))
    step("q2")
    step("q1")
    end("qkv", 3 * TILE, ("q1", 2 * TILE, 0, 0), ("q2", TILE, 2 * TILE, 0))
    sizes = [model, model, model, model, ff, model]
    if fast:
        cuts, at = [], 0
        for size in sizes:
            cuts.append(lax.dynamic_slice(state["small"], (0, at + device * (size // n)), (1, size // n)).reshape(size // n))
            at += size
    else:
        scatter = lambda g: lax.psum_scatter(g, AXES, scatter_dimension=0, tiled=True)
        factors = dict(qkv=(n1, d_mixed), proj=(att, branch), up=(n2, d_pre), down=(hidden, cot))
        grads = {k: scatter(dot_tn(*ab)) for k, ab in factors.items()}
        cuts, at = [], 0
        for size in sizes:
            cuts.append(scatter(small[0, at : at + size]))
            at += size
    shape = (rows, span, model)
    return (
        layer_out.reshape(shape), grad_tokens.reshape(shape), cuts[0], cuts[1], grads["qkv"], grads["proj"],
        cuts[2], cuts[3], grads["up"], cuts[4], grads["down"], cuts[5],
    )


def solution(mesh):
    wide, row, whole = P("rows", "seq", None), P(AXES), P()
    in_specs = (wide, P("rows", None), *[whole] * 10, wide)
    out_specs = (wide, wide, *[row] * 10)
    body = functools.partial(local, n_rows=mesh.shape["rows"], n_seq=mesh.shape["seq"])
    return jax.shard_map(body, mesh=mesh, in_specs=in_specs, out_specs=out_specs, check_vma=False)
```

```python
import functools

import jax
import jax.numpy as jnp
from jax import lax
from jax.experimental import pallas as pl
from jax.experimental.pallas import tpu as pltpu
from jax.sharding import PartitionSpec as P

HEADS = 16
EPS = 1e-05
BF, F32 = jnp.bfloat16, jnp.float32
AXES = ("rows", "seq")
DOWN = (1, 3)
STEPS = (
    "turn", "d1o", "d2o", "d1m", "dn2", "d2m", "n2t", "uo", "d1f", "mixer", "d1f", "merge", "um", "layer", "d2f",
    "d1f", "back", "att", "q1o", "d1f", "d2f", "d1a", "uf", "q1m", "po", "d2f", "q2o", "pm", "dn1", "q2m", "d2f",
    "q1f", "de", "small", "uf", "pf", "small", "q2f", "small", "uf", "pf", "small", "q1f", "small", "q2f", "small",
    "pf", "q1f", "q2f", "uf", "ue", "pf", "pe", "q2f", "q1f", "qe",
)
SUMS = 64
DEPTH = 80
TILE = 512
BEAT = 3


def dot(a, b):
    return jnp.dot(a, b, preferred_element_type=F32)


def dot_nt(a, b):
    return lax.dot_general(a, b, (((1,), (1,)), ((), ())), preferred_element_type=F32)


def dot_tn(a, b):
    return lax.dot_general(a, b, (((0,), (0,)), ((), ())), preferred_element_type=F32)


def iota(shape, dim):
    return lax.broadcasted_iota(jnp.int32, shape, dim)


SMEM = pl.BlockSpec(memory_space=pltpu.SMEM)
WHOLE = pl.BlockSpec(memory_space=pltpu.VMEM)
HBM = pl.BlockSpec(memory_space=pltpu.HBM)


def cut(at, size):
    return pl.ds(pl.multiple_of(at, size), size)


def in_vmem(x):
    return pltpu.with_memory_space_constraint(x, pltpu.VMEM)


def kernel_call(body, scalars, args, outs, scratch=(), far=(), hold=(), fetch=(), time=0.5, limit=4):
    n_in, n_hold, n_fetch, n_out = len(scalars) + len(args) + len(far), len(hold), len(fetch), len(outs)
    every = [(*o, True)[:3] for o in outs]
    every += [(f.shape, f.dtype, True) for f in fetch] + [((8, 128), F32, True)]

    def wrapped(*refs):
        ins, rest = refs[:n_in], refs[n_in + n_hold :]
        sources, rest = rest[:n_fetch], rest[n_fetch:]
        results, targets = rest[:n_out], rest[n_out : n_out + n_fetch]
        token, rest = rest[n_out + n_fetch], rest[n_out + n_fetch + 1 :]
        copies = []
        if n_fetch:
            sems, rest = rest[-1], rest[:-1]
            copies = [pltpu.make_async_copy(a, b, sems.at[k]) for k, (a, b) in enumerate(zip(sources, targets))]
        for copy in copies:
            copy.start()
        token[...] = jnp.zeros_like(token)
        body(*ins, *results, *rest)
        for copy in copies:
            copy.wait()

    shapes = [pltpu.VMEM(s, d) if v else jax.ShapeDtypeStruct(s, d) for s, d, v in every]
    in_hbm = lambda x: pltpu.with_memory_space_constraint(x, pltpu.HBM)
    out = pl.pallas_call(
        wrapped,
        name=body.__qualname__.split(".")[0],
        in_specs=[SMEM] * len(scalars)
        + [WHOLE] * len(args)
        + [HBM] * len(far)
        + [WHOLE] * n_hold
        + [HBM] * n_fetch,
        out_specs=[WHOLE] * len(every),
        out_shape=shapes,
        scratch_shapes=[*scratch, *([pltpu.SemaphoreType.DMA((n_fetch,))] if n_fetch else [])],
        compiler_params=pltpu.CompilerParams(vmem_limit_bytes=limit << 20),
        cost_estimate=pl.CostEstimate(flops=int(time * 1e10), bytes_accessed=1, transcendentals=0),
    )(*scalars, *map(in_vmem, args), *map(in_hbm, far), *map(in_vmem, hold), *map(in_hbm, fetch))
    return out


def normal(x):
    center = x - jnp.mean(x, -1, keepdims=True)
    root = lax.rsqrt(jnp.mean(center * center, -1, keepdims=True) + EPS)
    return center * root, root


def feature(u):
    return jnp.where(u > 0, u + 1.0, jnp.exp(jnp.minimum(u, 0.0)))


def keep_from(lb, row, span):
    last = 0 - span
    for k in range(lb.shape[1]):
        last = jnp.where(lb[row, k] < span, jnp.maximum(last, lb[row, k]), last)
    return last


def carry_to(lb, row, span):
    end = span
    for k in range(lb.shape[1]):
        end = jnp.where(lb[row, k] >= 0, jnp.minimum(end, lb[row, k]), end)
    return end


def block_mask(lb, row, span):
    t, s = iota((span, span), 0), iota((span, span), 1)
    ok = s <= t
    for k in range(lb.shape[1]):
        ok = ok & ((lb[row, k] > t) | (s >= lb[row, k]))
    return ok.astype(F32)


def pack_state(m):
    half = m.shape[0] // 2
    return jnp.where(iota((half, m.shape[1]), 1) < half, m[:half], m[half:])


def unpack_state(c):
    half = c.shape[0]
    left = iota(c.shape, 1) < half
    return jnp.concatenate([jnp.where(left, c, 0.0), jnp.where(left, 0.0, c)], 0)


def split(x):
    hi = x.astype(BF)
    return hi, (x - hi.astype(F32)).astype(BF)


def head_ones(lanes=128):
    half = lanes // 2
    return ((iota((lanes, lanes), 0) < half) == (iota((lanes, lanes), 1) < half)).astype(BF)


def head_sum(x):
    hi, lo = split(x)
    ones = head_ones(x.shape[1])
    return dot(jnp.concatenate([hi, lo], 1), jnp.concatenate([ones, ones], 0))


def dot_split(a, m):
    hi, lo = split(m)
    return dot(jnp.concatenate([a, a], 1), jnp.concatenate([hi, lo], 0))


def keys_values(lb, tokens, vectors, w_qkv, span, **kw):
    count, model = tokens.shape
    rows, width = count // span, 256
    n_vec, blocks = len(vectors), model // 512

    def body(lb, *refs):
        x_in, vec_in, w_in = refs[0], refs[1 : 1 + n_vec], refs[1 + n_vec]
        n1, km, v, own, *vecs = refs[2 + n_vec : 6 + 2 * n_vec]
        x, w, sems = refs[6 + 2 * n_vec :]

        def copy(k, a, b):
            return pltpu.make_async_copy(a, b, sems.at[k])

        def columns(j):
            lanes = slice(j * 512, (j + 1) * 512)
            return copy(1 + n_vec + j, w_in.at[:, model + j * 512 : model + (j + 1) * 512], w.at[:, lanes])

        head = [copy(0, x_in, x)] + [copy(1 + k, a, b) for k, (a, b) in enumerate(zip(vec_in, vecs))]
        for c in head:
            c.start()
        for c in [c for j in range(blocks) for c in (j, blocks + j)]:
            columns(c).start()
        for c in head:
            c.wait()

        @pl.loop(0, count // 64, unroll=2)
        def _(i):
            at = cut(i * 64, 64)
            n1[at] = (normal(x[at].astype(F32))[0] * vecs[0][...] + vecs[1][...]).astype(BF)

        kept = [iota((span, width), 0) >= keep_from(lb, r, span) for r in range(rows)]
        for j in range(model // width):
            if j * width % 512 == 0:
                columns(j * width // 512).wait()
                columns(blocks + j * width // 512).wait()
            lanes = slice(j * width, (j + 1) * width)
            key = feature(dot(n1[...], w[:, lanes])).astype(BF)
            val = dot(n1[...], w[:, model + j * width : model + (j + 1) * width]).astype(BF)
            km[:, lanes], v[:, lanes] = key, val
            for r in range(rows):
                part = slice(r * span, (r + 1) * span)
                owned = jnp.where(kept[r], key[part], jnp.zeros((), BF))
                for p in range(width // 128):
                    at = slice(p * 128, (p + 1) * 128)
                    block = j * (width // 128) + p
                    own[r, block, 0:SUMS] = pack_state(dot_tn(owned[:, at], val[part, at])).astype(BF)
                    total = jnp.sum(owned[:, at].astype(F32), 0, keepdims=True)
                    own[r, block, SUMS:DEPTH] = jnp.broadcast_to(total, (DEPTH - SUMS, 128)).astype(BF)

    wide = ((count, model), BF)
    outs = [wide, wide, wide, ((rows, model // 128, DEPTH, 128), BF)]
    outs += [(v.shape, v.dtype) for v in vectors]
    return kernel_call(
        body, (lb,), (), outs, far=(tokens, *vectors, w_qkv),
        scratch=[
            pltpu.VMEM((count, model), BF),
            pltpu.VMEM((model, 2 * model), BF),
            pltpu.SemaphoreType.DMA((1 + n_vec + 2 * blocks,)),
        ],
        limit=7, time=7.3, **kw,
    )


def merge_states(coefs, own, got, **kw):
    rows = own.shape[0]

    def body(c, a, b, out):
        for r in range(rows):
            out[r] = (c[0, r] * a[r].astype(F32) + c[1, r] * b[r].astype(F32)).astype(BF)

    return kernel_call(body, (coefs,), (own, got), [(own.shape, BF)], **kw)


def queries(normed, w_qkv, tables, shards, **kw):
    count, model = normed.shape
    tiles = model // TILE

    def body(tables, n, w_in, q, n_t, w, sems):
        copies = [
            pltpu.make_async_copy(w_in.at[:, j * TILE : (j + 1) * TILE], w.at[:, j * TILE : (j + 1) * TILE], sems.at[j])
            for j in range(tiles)
        ]
        for c in copies:
            c.start()
        turn(tables, n, n_t, model // shards)
        for j in range(tiles):
            lanes = slice(j * TILE, (j + 1) * TILE)
            copies[j].wait()
            q[:, lanes] = feature(dot(n[...], w[:, lanes])).astype(BF)

    return kernel_call(
        body, (tables,), (normed,), [((count, model), BF), ((model, count), BF)], far=(w_qkv,),
        scratch=[pltpu.VMEM((model, model), BF), pltpu.SemaphoreType.DMA((tiles,))],
        limit=5, time=3.9, **kw,
    )


def active_grads(cotangent, w_down, **kw):
    count, model = cotangent.shape
    ff = w_down.shape[0]

    def body(c, w, out):
        for j in range(ff // TILE):
            lanes = slice(j * TILE, (j + 1) * TILE)
            out[:, lanes] = dot_nt(c[...], w[lanes, :]).astype(BF)

    return kernel_call(
        body, (), (cotangent, w_down), [((count, ff), BF)], time=4.5, **kw
    )


def attend_inside(lb, query, key, values, span, **kw):
    count, model = query.shape
    rows = count // span

    def body(lb, q_ref, k_ref, v_ref, numer, denom, mask):
        for r in range(rows):
            mask[r] = block_mask(lb, r, span)
        left = iota((span, 128), 1) < 64
        zero = jnp.zeros((), BF)

        @pl.loop(0, model // 128, unroll=4)
        def _(p):
            lanes = cut(p * 128, 128)
            for r in range(rows):
                part = slice(r * span, (r + 1) * span)
                q, k, v = q_ref[part, lanes], k_ref[part, lanes], v_ref[part, lanes]
                total = 0.0
                for e in range(2):
                    mine = left if e == 0 else ~left
                    scores = dot_nt(jnp.where(mine, q, zero), k)
                    weights = (scores * mask[r]).astype(BF)
                    both = jnp.concatenate([jnp.where(mine, v, zero), mine.astype(BF)], 1)
                    total = total + dot(weights, both)
                numer[part, lanes] = total[:, :128]
                denom[part, lanes] = total[:, 128:]

    wide = ((count, model), F32)
    return kernel_call(
        body, (lb,), (query, key, values), [wide, wide],
        scratch=[pltpu.VMEM((rows, span, span), F32)], time=5.7, **kw,
    )


def state_of(coefs, gots, r, p):
    total = 0.0
    for i, got in enumerate(gots):
        total = total + coefs[i, r] * got[r, p].astype(F32)
    return total


def attend_join(lb, coefs, gots, query, numer, denom, tokens, w_proj, gain, bias, span, **kw):
    count, model = query.shape
    pairs, n = model // 128, len(gots)
    rows = count // span

    def body(lb, coefs, *refs):
        gots, (q_ref, num_ref, den_ref, x, w, g, b, att, rden, middle, n2) = refs[:n], refs[n:]
        place = iota((span, 128), 0)

        @pl.loop(0, pairs, unroll=4)
        def _(p):
            lanes = cut(p * 128, 128)
            for r in range(rows):
                part = slice(r * span, (r + 1) * span)
                state = state_of(coefs, gots, r, p)
                q = jnp.where(place < carry_to(lb, r, span), q_ref[part, lanes], jnp.zeros((), BF))
                num = num_ref[part, lanes] + dot_split(q, unpack_state(state[0:SUMS]))
                den = den_ref[part, lanes] + head_sum(q.astype(F32) * state[SUMS : SUMS + 1])
                inv = 1.0 / den
                rden[part, lanes] = inv
                att[part, lanes] = (num * inv).astype(BF)

        for j in range(model // 256):
            lanes = slice(j * 256, (j + 1) * 256)
            middle[:, lanes] = x[:, lanes].astype(F32) + dot(att[...], w[:, lanes])

        @pl.loop(0, count // 64, unroll=2)
        def _(i):
            at = cut(i * 64, 64)
            n2[at] = (normal(middle[at])[0] * g[...] + b[...]).astype(BF)

    wide = (count, model)
    return kernel_call(
        body, (lb, coefs), (*gots, query, numer, denom, tokens, w_proj, gain, bias),
        [(wide, BF), (wide, F32), (wide, F32), (wide, BF)],
        time=5.0, **kw,
    )


def expand(normed, w_up, up_bias, d_active, **kw):
    count, model = normed.shape
    ff = w_up.shape[1]
    c0, c1 = 0.7978845608028654, 0.7978845608028654 * 0.044715
    step = 32

    def body(n, w, b, da, hid, dp, total, even, odd):
        ones = jnp.ones((16, count), BF)

        def product(j, out):
            out[...] = dot(n[...], w[:, cut(j * TILE, TILE)])

        def rest(j, u_ref):
            lanes = cut(j * TILE, TILE)
            bias = b[:, lanes]
            for i in range(count // step):
                at = slice(i * step, (i + 1) * step)
                u = u_ref[at] + bias
                z = u * (c0 + c1 * (u * u))
                t = jnp.tanh(z)
                rise = 0.5 + 0.5 * t
                hid[at, lanes] = (u * rise).astype(BF)
                slope = rise * (1.0 + (1.0 - t) * (3.0 * z - (2.0 * c0) * u))
                dp[at, lanes] = (slope * da[at, lanes].astype(F32)).astype(BF)
            total[:, lanes] = dot(ones, dp[:, lanes])[0:1]

        tiles = ff // TILE
        product(0, even)

        @pl.loop(0, tiles // 2 - 1)
        def _(i):
            product(2 * i + 1, odd)
            rest(2 * i, even)
            product(2 * i + 2, even)
            rest(2 * i + 1, odd)

        product(tiles - 1, odd)
        rest(tiles - 2, even)
        rest(tiles - 1, odd)

    wide = ((count, ff), BF)
    return kernel_call(
        body, (), (normed, w_up, up_bias, d_active), [wide, wide, ((1, ff), F32)],
        scratch=[pltpu.VMEM((count, TILE), F32)] * 2, limit=6, time=11.0, **kw,
    )


def turn(tables, x, out, deep):
    for j in range(x.shape[1] // 128):
        t = x[:, j * 128 : (j + 1) * 128].T
        for k in range(128 // deep):
            out[cut(tables[2, j * (128 // deep) + k] * deep, deep), :] = t[k * deep : (k + 1) * deep]


def turned(x, tables, shards, **kw):
    count, model = x.shape
    deep = model // shards

    def body(tables, x, out):
        turn(tables, x, out, deep)

    return kernel_call(body, (tables,), (x,), [((model, count), BF)], **kw)


def weight_grad(lhs_t, rhs, first, steps, side, tables, got=None, **kw):
    deep, count = lhs_t.shape
    shards = tables.shape[1]
    rows, half = deep // shards, deep // 2
    time = 0.9 * steps
    shape = (deep, TILE * steps)

    def tile(b, which, j):
        return b[:, cut((which * side + first + j) * TILE, TILE)]

    if got is None:

        def body(tables, a, b, out):
            for j in range(steps):
                total = dot(a[...], tile(b, 1 - tables[3, 0], j)).astype(BF)
                for k in range(shards):
                    at = (k & 0b01010) | (k >> 4 & 1) << 2 | (k >> 2 & 1) << 4 | (~k & 1)
                    out[at * rows : (at + 1) * rows, j * TILE : (j + 1) * TILE] = total[k * rows : (k + 1) * rows]

        return kernel_call(body, (tables,), (lhs_t, rhs), [(shape, BF)], time=time, **kw)

    def body(tables, a, b, g, send, keep):
        for j in range(steps):
            lanes = slice(j * TILE, (j + 1) * TILE)
            total = dot(a[...], tile(b, tables[3, 0], j)) + g[:, lanes].astype(F32)
            send[:, lanes] = total[:half].astype(BF)
            keep[:, lanes] = total[half:].astype(BF)

    return kernel_call(
        body, (tables,), (lhs_t, rhs, got), [((half, TILE * steps), BF)] * 2, limit=9, time=time, **kw
    )


def transposed(x, **kw):
    def body(x, out):
        for j in range(x.shape[1] // TILE):
            out[j * TILE : (j + 1) * TILE, :] = x[:, j * TILE : (j + 1) * TILE].T

    return kernel_call(body, (), (x,), [(x.shape[::-1], x.dtype)], time=2.0, **kw)


def down_grad(hidden_t, cotangent, width, first, side, tables, got=None, **kw):
    ff, count = hidden_t.shape
    shards = tables.shape[1]
    deep = ff // shards
    per = TILE // deep
    steps = ff // TILE
    time = width / 110

    def product(tables, h, c, i, mine):
        which = 0 if mine else 1
        core = tables[3, 0]
        column = pl.multiple_of((core if mine else 1 - core) * side + first, 128)
        lhs = [h[cut(tables[which, per * i + k] * deep, deep), :] for k in range(per)]
        return dot(jnp.concatenate(lhs, 0), c[:, pl.ds(column, width)])

    if got is None:

        def body(tables, h, c, out):
            for i in range(steps):
                out[i * TILE : (i + 1) * TILE] = product(tables, h, c, i, False).astype(BF)

        return kernel_call(body, (tables,), (hidden_t, cotangent), [((ff, width), BF)], time=time, **kw)

    def body(tables, h, c, g, send, keep):
        for i in range(steps):
            total = product(tables, h, c, i, True) + g[i * TILE : (i + 1) * TILE].astype(F32)
            out, at = (send, i) if i < steps // 2 else (keep, i - steps // 2)
            out[at * TILE : (at + 1) * TILE] = total.astype(BF)

    return kernel_call(
        body, (tables,), (hidden_t, cotangent, got), [((ff // 2, width), BF)] * 2, limit=6, time=time, **kw
    )


def norm_grad_rows(e_ref, x_of, gain, count, write):
    step, model = 32, gain.shape[1]

    def one(i, sums):
        at = cut(i * step, step)
        e = e_ref[at]
        hat, root = normal(x_of(at))
        g = e * gain[...]
        back = root * (g - jnp.mean(g, -1, keepdims=True) - hat * jnp.mean(g * hat, -1, keepdims=True))
        write(at, back)
        eights = lambda v: jnp.sum(v.reshape(step // 8, 8, model), 0)
        return sums[0] + eights(e * hat), sums[1] + eights(e)

    zero = jnp.zeros((8, model), F32)
    sums = lax.fori_loop(0, count // step, one, (zero, zero), unroll=4)
    return [jnp.sum(s, 0, keepdims=True) for s in sums]


def second_norm_grads(d_pre, w_up, middle, cotangent, gain, **kw):
    count, ff = d_pre.shape
    model = w_up.shape[0]

    def body(d, w, mid, cot, g, d_mid, branch, g_gain, g_bias, g_down, e):
        for j in range(model // 256):
            lanes = slice(j * 256, (j + 1) * 256)
            e[:, lanes] = dot_nt(d[...], w[lanes, :])

        def write(at, back):
            out = cot[at].astype(F32) + back
            d_mid[at] = out
            branch[at] = out.astype(BF)

        g_gain[...], g_bias[...] = norm_grad_rows(e, lambda at: mid[at], g, count, write)
        g_down[...] = jnp.sum(cot[...].astype(F32), 0, keepdims=True)

    vec, wide = ((1, model), F32), (count, model)
    return kernel_call(
        body, (), (d_pre, w_up, middle, cotangent, gain), [(wide, F32), (wide, BF), vec, vec, vec],
        scratch=[pltpu.VMEM(wide, F32)], time=7.0, **kw,
    )


def mixer_grads(lb, branch, w_proj, attended, rden, query, span, **kw):
    count, model = branch.shape
    rows, pairs = count // span, model // 128

    def body(lb, br, w, att, rd, q_ref, dn, dd, own):
        place = iota((span, 128), 0)
        for j in range(model // 256):
            d_att = dot_nt(br[...], w[j * 256 : (j + 1) * 256, :])
            for k in range(2):
                p = 2 * j + k
                lanes = slice(p * 128, (p + 1) * 128)
                for r in range(rows):
                    part = slice(r * span, (r + 1) * span)
                    d, inv = d_att[part, k * 128 : (k + 1) * 128], rd[part, lanes]
                    d_den = -head_sum(d * att[part, lanes].astype(F32)) * inv
                    d_num = (d * inv).astype(BF)
                    dn[part, lanes], dd[part, lanes] = d_num, d_den
                    q = jnp.where(place < carry_to(lb, r, span), q_ref[part, lanes], jnp.zeros((), BF))
                    own[r, p, 0:SUMS] = pack_state(dot_tn(q, d_num)).astype(BF)
                    total = jnp.sum(d_den * q.astype(F32), 0, keepdims=True)
                    own[r, p, SUMS:DEPTH] = jnp.broadcast_to(total, (DEPTH - SUMS, 128)).astype(BF)

    wide = (count, model)
    return kernel_call(
        body, (lb,), (branch, w_proj, attended, rden, query),
        [(wide, BF), (wide, F32), ((rows, pairs, DEPTH, 128), BF)],
        time=5.0, **kw,
    )


def attend_back(lb, coefs, back_coefs, gots, back_gots, query, key, values, d_num, d_den, span, **kw):
    count, model = query.shape
    rows, n, m = count // span, len(gots), len(back_gots)

    def body(lb, coefs, back_coefs, *refs):
        gots, back_gots = refs[:n], refs[n : n + m]
        q_ref, k_ref, v_ref, dn_ref, dd_ref, out, mask, mask_t = refs[n + m :]
        for r in range(rows):
            ok = block_mask(lb, r, span)
            mask[r], mask_t[r] = ok, ok.T
        lane, place = iota((span, 128), 1), iota((span, 128), 0)
        left = lane < 64
        zero = jnp.zeros((), BF)

        @pl.loop(0, model // 128, unroll=4)
        def _(p):
            lanes = cut(p * 128, 128)
            for r in range(rows):
                part = slice(r * span, (r + 1) * span)
                carried = place < carry_to(lb, r, span)
                kept = place >= keep_from(lb, r, span)
                q, k, v = q_ref[part, lanes], k_ref[part, lanes], v_ref[part, lanes]
                dn, dd = dn_ref[part, lanes], dd_ref[part, lanes]
                hi, lo = split(dd)
                v_ones = jnp.concatenate([v, jnp.ones_like(v)], 1)
                dq = dk = dv = 0.0
                for e in range(2):
                    mine = left if e == 0 else ~left
                    at = 64 * e
                    qm, dnm = jnp.where(mine, q, zero), jnp.where(mine, dn, zero)
                    extra = jnp.where(lane == at, hi, jnp.where(lane == at + 1, lo, zero))
                    dn_den = jnp.concatenate([dnm, extra], 1)
                    ds = (dot_nt(dn_den, v_ones) * mask[r]).astype(BF)
                    w_t = (dot_nt(k, qm) * mask_t[r]).astype(BF)
                    dq = dq + dot(ds, jnp.where(mine, k, zero))
                    dk = dk + dot_tn(ds, qm)
                    dv = dv + dot(w_t, dnm)
                state, own = state_of(coefs, gots, r, p), state_of(back_coefs, back_gots, r, p)
                s_hi, s_lo = split(unpack_state(state[0:SUMS]))
                o_hi, o_lo = split(unpack_state(own[0:SUMS]))
                through_s = dot_nt(jnp.concatenate([dn, dn], 1), jnp.concatenate([s_hi, s_lo], 1))
                through_o = dot_nt(jnp.concatenate([v, v], 1), jnp.concatenate([o_hi, o_lo], 1))
                through_k = dot(jnp.concatenate([k, k], 1), jnp.concatenate([o_hi, o_lo], 0))
                dq = dq + jnp.where(carried, through_s + dd * state[SUMS : SUMS + 1], 0.0)
                dk = dk + jnp.where(kept, through_o + own[SUMS : SUMS + 1], 0.0)
                dv = dv + jnp.where(kept, through_k, 0.0)
                out[part, lanes] = (dq * jnp.minimum(q.astype(F32), 1.0)).astype(BF)
                out[part, cut(model + p * 128, 128)] = (dk * jnp.minimum(k.astype(F32), 1.0)).astype(BF)
                out[part, cut(2 * model + p * 128, 128)] = dv.astype(BF)

    return kernel_call(
        body, (lb, coefs, back_coefs), (*gots, *back_gots, query, key, values, d_num, d_den),
        [((count, 3 * model), BF)],
        scratch=[pltpu.VMEM((rows, span, span), F32)] * 2, time=12.0, **kw,
    )


def first_norm_grads(d_mixed, w_qkv, tokens, d_middle, gain, others, **kw):
    count = d_mixed.shape[0]
    model = w_qkv.shape[0]

    n = len(others)

    def body(d, x, dm, g, *refs):
        rest, (w_in, out, packed, e, w, sems) = refs[:n], refs[n:]
        tiles = model // 256

        def copy(j):
            return pltpu.make_async_copy(w_in.at[j * 256 : (j + 1) * 256, :], w.at[j % 2], sems.at[j % 2])

        copy(0).start()
        for j in range(tiles):
            copy(j).wait()
            if j + 1 < tiles:
                copy(j + 1).start()
            e[:, j * 256 : (j + 1) * 256] = dot_nt(d[...], w[j % 2])

        def write(at, back):
            out[at] = dm[at] + back

        at = 0
        for part in (*norm_grad_rows(e, lambda at: x[at].astype(F32), g, count, write), *[r[...] for r in rest]):
            packed[:, at : at + part.shape[1]] = part
            at += part.shape[1]

    wide, size = (count, model), 2 * model + sum(o.shape[1] for o in others)
    return kernel_call(
        body, (), (d_mixed, tokens, d_middle, gain, *others), [(wide, F32, False), ((1, size), F32)], far=(w_qkv,),
        scratch=[
            pltpu.VMEM(wide, F32), pltpu.VMEM((2, 256, w_qkv.shape[1]), BF), pltpu.SemaphoreType.DMA((2,))
        ], limit=10, time=6.5, **kw,
    )


def layer_result(hidden, w_down, middle, down_bias, **kw):
    count, ff = hidden.shape
    model, tiles = w_down.shape[1], 8
    deep = ff // tiles

    def body(h, mid, b, w_in, out, w, total, sems):
        def copy(j):
            return pltpu.make_async_copy(w_in.at[j * deep : (j + 1) * deep, :], w.at[j % 3], sems.at[j % 3])

        copy(0).start()
        copy(1).start()
        for j in range(tiles):
            copy(j).wait()
            if j + 2 < tiles:
                copy(j + 2).start()
            part = dot(h[:, j * deep : (j + 1) * deep], w[j % 3])
            if j == 0:
                total[...] = mid[...] + b[...] + part
            elif j < tiles - 1:
                total[...] += part
            else:
                out[...] = (total[...] + part).astype(BF)

    return kernel_call(
        body, (), (hidden, middle, down_bias), [((count, model), BF, False)], far=(w_down,),
        scratch=[pltpu.VMEM((3, deep, model), BF), pltpu.VMEM((count, model), F32), pltpu.SemaphoreType.DMA((3,))],
        time=5.5, limit=9, **kw,
    )


def swap(v, pairs):
    return lax.ppermute(v, AXES, pairs)


def state_plan(doc_end, n_rows, n_seq, later=False):
    me = lax.axis_index("seq")

    def reaches(a, b):
        def at(i):
            return lax.dynamic_index_in_dim(doc_end, i, 1, keepdims=False)

        return (at(a) == at(b)).astype(F32)

    pairs, merges, coefs = [], [], []
    size = 1
    while size < n_seq:
        step = [(r * n_seq + s, r * n_seq + (s ^ size)) for r in range(n_rows) for s in range(n_seq)]
        if 2 * size == n_seq:
            step = [p for p in step if bool(p[0] % n_seq & size) == later]
        pairs.append(step)
        upper = (me // size) % 2 == 1
        low = me // (2 * size) * (2 * size)
        mid, high = low + size, low + 2 * size
        if later:
            coefs.append(jnp.where(upper, 0.0, reaches(me + 1, mid)))
            same = reaches(low, mid)
            merges.append(jnp.stack([jnp.where(upper, same, 1.0), jnp.where(upper, 1.0, same)]))
        else:
            coefs.append(jnp.where(upper, reaches(mid, me), 0.0))
            same = reaches(mid, high)
            merges.append(jnp.stack([jnp.where(upper, 1.0, same), jnp.where(upper, same, 1.0)]))
        size *= 2
    return pairs, merges, jnp.stack(coefs)


def stage_pairs(n_rows, n_seq):
    def pairs(bit0, bit1):
        return [(i, i ^ (bit1 if i & 1 else bit0)) for i in range(n_rows * n_seq)]

    return [pairs(2, 4), pairs(8, 8), pairs(4, 2), pairs(16, 16)]


def core_pairs(n):
    return [(i, i ^ 1) for i in range(n)]


def shard_tables(device):
    j = jnp.arange(32, dtype=jnp.int32)

    def bits(device):
        core = device & 1
        return jnp.where(core == 0, 1, 2), 3, jnp.where(core == 0, 2, 1), 4, 0

    def order(device):
        move = 0
        for k, at in enumerate(bits(device)):
            move = move | (((31 - j) >> (4 - k)) & 1) << at
        return device ^ move

    place = 0
    for k, at in enumerate(bits(device)):
        place = place | (1 - (((j ^ device) >> at) & 1)) << (4 - k)
    return jnp.stack([order(device), order(device ^ 1), place, jnp.broadcast_to(device & 1, (32,))])


def fold(parts, **kw):
    rows = parts[0][0].shape[0]
    widths = [k.shape[1] for k, g in parts]
    half, step, n = rows // 2, min(32, rows // 2), len(parts)

    def body(*refs):
        send, keep = refs[2 * n :]

        @pl.loop(0, half // step, unroll=min(2, half // step))
        def _(i):
            at = 0
            top, low = cut(i * step, step), cut(half + i * step, step)
            for k, w in enumerate(widths):
                a, b = refs[2 * k], refs[2 * k + 1]
                lanes = slice(at, at + w)
                send[top, lanes] = (a[top].astype(F32) + b[top].astype(F32)).astype(BF)
                keep[top, lanes] = a[low].astype(F32) + b[low].astype(F32)
                at += w

    shape = (half, sum(widths))
    return kernel_call(body, (), [x for p in parts for x in p], [(shape, BF), (shape, F32)], **kw)


def place(tables, pieces, side, **kw):
    rows = pieces[0][0].shape[0]

    def body(tables, *refs):
        core, out = tables[3, 0], refs[-1]
        for k, (mine, got, at, w, to) in enumerate(pieces):
            out[:, pl.ds(pl.multiple_of(core * side + to, 128), w)] = refs[2 * k][:, at : at + w]
            out[:, pl.ds(pl.multiple_of((1 - core) * side + to, 128), w)] = refs[2 * k + 1][:, at : at + w].astype(F32)

    args = [x for p in pieces for x in p[:2]]
    return kernel_call(body, (tables,), args, [((rows, 2 * side), F32, False)], **kw)


def settle(a, **kw):
    def body(a, out):
        out[...] = a[...]

    return kernel_call(body, (), (a,), [(a.shape, a.dtype)], **kw)


def add(a, b, **kw):
    def body(a, b, out):
        out[...] = a[...] + b[...]

    return kernel_call(body, (), (a, b), [(a.shape, a.dtype)], **kw)


def local(
    tokens, bounds, norm1_gain, norm1_bias, w_qkv, w_proj, norm2_gain, norm2_bias,
    w_up, up_bias, w_down, down_bias, cotangent, n_rows, n_seq,
):
    rows, span, model = tokens.shape
    ff = w_up.shape[1]
    count, n = rows * span, n_rows * n_seq
    seq = lax.axis_index("seq")
    device = lax.axis_index("rows") * n_seq + seq
    core = device & 1
    lb = bounds - seq * span
    ends = jnp.arange(n_seq + 1, dtype=jnp.int32) * span - 1
    doc_end = jnp.sum((bounds[:, None, :] <= ends[None, :, None]).astype(jnp.int32), -1)
    x, cot = tokens.reshape(count, model), cotangent.reshape(count, model)
    vectors = [v.reshape(1, -1) for v in (norm1_gain, norm1_bias, norm2_gain, norm2_bias, up_bias, down_bias)]
    shards = 32
    fast = n == shards and model % (shards * 32) == 0 and ff % (shards * 128) == 0
    tables = shard_tables(device)
    plan = state_plan(doc_end, n_rows, n_seq)
    back_plan = state_plan(doc_end, n_rows, n_seq, later=True)
    held, last, ran, beats = [], [], [], []

    def run(kernel, *args, **kw):
        used = {id(x) for x in jax.tree.leaves(args)}
        small = kernel in (fold, settle, add, merge_states, turned)
        beat = beats and len(ran) % BEAT == 0 and "small" not in state
        extra = beats[:] if beat else []
        kept = [] if small else [x for x in held if id(x) not in used]
        *outs, token = kernel(*args, hold=kept + last + extra, **kw)
        last[:] = [token]
        ran.append(kernel)
        if beat:
            beats[:] = [swap(token, core_pairs(n))]
        return outs[0] if len(outs) == 1 else outs

    def keep(*arrays):
        held.extend(arrays)

    def drop(*arrays):
        held[:] = [x for x in held if all(x is not y for y in arrays)]

    def merged(plan, gots, own):
        return run(merge_states, plan[1][len(gots) - 1], own, gots[-1])

    n1, km, v, own, *vectors = run(keys_values, lb, x, vectors, w_qkv, span)
    gain1, bias1, gain2, bias2, b_up, b_down = vectors
    keep(gain1, gain2, bias2, b_up, b_down)
    gots = [swap(own, plan[0][0])]
    qm, n1_t = run(queries, n1, w_qkv, tables, shards)
    group = own
    for pairs in plan[0][1:]:
        group = merged(plan, gots, group)
        gots.append(swap(group, pairs))
    numer, denom, wdown_v, wproj_v, cot_v = run(attend_inside, lb, qm, km, v, span, fetch=(w_down, w_proj, cot))
    drop(km, v, qm)
    keep(numer, denom, wproj_v, cot_v)
    d_act = run(active_grads, cot_v, wdown_v)
    keep(d_act)
    att, rden, middle, n2, wup_v = run(
        attend_join, lb, plan[2], gots, qm, numer, denom, x, wproj_v, gain2, bias2, span, fetch=(w_up,)
    )
    drop(numer, denom, wproj_v)
    keep(wup_v, n2)
    hidden, d_pre, g_up_bias = run(expand, n2, wup_v, b_up, d_act)
    drop(d_act)
    keep(hidden, d_pre)

    stages = [*stage_pairs(n_rows, n_seq), core_pairs(n)] if fast else []
    state = {}

    def other(name, kernel, *args):
        if fast:
            out = run(kernel, *args, tables)
            state[name] = (kernel, args, swap(out, core_pairs(n)))

    def mine(name):
        if fast:
            kernel, args, got = state[name]
            send, kept = run(kernel, *args, tables, got)
            state[name] = (kept, swap(send, stages[0]), 1)

    def step(name, *names):
        if fast:
            parts = [state[k] for k in names or (name,)]
            send, kept = run(fold, [p[:2] for p in parts])
            at = parts[0][2]
            state[name] = (kept, swap(send, stages[at]), at + 1)

    def end(to, side, *pieces):
        if fast:
            found = []
            for name, w, column, at in pieces:
                kept, got, unused = state[name]
                found.append((kept, got, at, w, column))
            grads[to] = run(place, tables, found, side)

    def arrived(name):
        if fast:
            kept, got, at = state[name]
            state[name] = (kept, run(settle, got), at)

    grads, small_step, box = {}, [0], {}
    half = ff // TILE // 2
    widths = [w * model // 2 // sum(DOWN) for w in DOWN]

    def small_sum():
        k = small_step[0]
        if k:
            state["small"] = run(add, state["small"], state["small got"])
        if k < 5:
            state["small got"] = swap(state["small"], [(i, i ^ (1 << k)) for i in range(n)])
        small_step[0] += 1

    def second_norm():
        box["d_mid"], box["branch"], *box["sums"], box["w_proj"] = run(
            second_norm_grads, d_pre, wup_v, middle, cot_v, gain2, fetch=(w_proj,)
        )

    def mixer():
        box["d_num"], box["d_den"], box["group"] = run(
            mixer_grads, lb, box["branch"], box["w_proj"], att, rden, qm, span
        )
        box["gots"] = [swap(box["group"], back_plan[0][0])]

    def merge():
        for pairs in back_plan[0][1:]:
            box["group"] = merged(back_plan, box["gots"], box["group"])
            box["gots"].append(swap(box["group"], pairs))

    def back():
        box["d_mixed"] = run(
            attend_back, lb, plan[2], back_plan[2], gots, box["gots"], qm, km, v,
            box["d_num"], box["d_den"], span,
        )

    def first_norm():
        g_gain2, g_bias2, g_down_bias = box["sums"]
        others = [g_gain2, g_bias2, g_up_bias, g_down_bias]
        box["grad_tokens"], state["small"] = run(
            first_norm_grads, box["d_mixed"], w_qkv, x, box["d_mid"], gain1, others
        )

    def layer():
        box["layer_out"] = run(layer_result, hidden, w_down, middle, b_down)

    def keep_as(name, *call):
        box[name] = run(*call)

    def down(k):
        return down_grad, box["hidden_t"], cot_v, widths[k], sum(widths[:k]), model // 2

    tasks = dict(
        dn2=second_norm, mixer=mixer, merge=merge, layer=layer, back=back, dn1=first_norm, small=small_sum,
        turn=lambda: keep_as("hidden_t", transposed, hidden),
        n2t=lambda: keep_as("n2_t", turned, n2, tables, shards),
        att=lambda: keep_as("att_t", turned, att, tables, shards),
        d1o=lambda: other("d1", *down(0)),
        d2o=lambda: other("d2", *down(1)),
        uo=lambda: other("u", weight_grad, box["n2_t"], d_pre, 0, half, half),
        po=lambda: other("p", weight_grad, box["att_t"], box["branch"], 0, 1, 1),
        q1o=lambda: other("q1", weight_grad, n1_t, box["d_mixed"], 0, 2, 3),
        q2o=lambda: other("q2", weight_grad, n1_t, box["d_mixed"], 2, 1, 3),
        d1a=lambda: arrived("d1"),
        de=lambda: end("down", model // 2, ("d1", widths[0], 0, 0), ("d2", widths[1], widths[0], 0)),
        ue=lambda: end("up", ff // 2, ("u", ff // 2, 0, 0)),
        pe=lambda: end("proj", model // 2, ("p", TILE, 0, 0)),
        qe=lambda: end("qkv", 3 * TILE, ("q1", 2 * TILE, 0, 0), ("q2", TILE, 2 * TILE, 0)),
    )
    for name in ("d1", "d2", "u", "p", "q1", "q2"):
        tasks[name + "m"] = functools.partial(mine, name)
        tasks[name + "f"] = functools.partial(step, name)
    pinned = dict(
        hidden=(lambda: hidden, ("turn",)), d_pre=(lambda: d_pre, ("uo", "um", "dn2",)), cot=(lambda: cot_v, ("d1o", "d2o", "d1m", "d2m", "dn2",)),
        w_up=(lambda: wup_v, ("dn2",)), n2=(lambda: n2, ("n2t",)), hidden_t=(lambda: box.get("hidden_t"), ("d1o", "d2o", "d1m", "d2m",)),
        w_proj=(lambda: box.get("w_proj"), ("mixer",)),
        d_mixed=(lambda: box.get("d_mixed"), ("q1o", "q2o", "q1m", "q2m", "dn1",)), gain2=(lambda: gain2, ("dn2",)), b_down=(lambda: b_down, ("layer",)),
        gain1=(lambda: gain1, ("dn1",)),
    )
    local_steps = ("dn2", "mixer", "merge", "layer", "back", "dn1")
    steps = [name for name in STEPS if fast or name in local_steps]
    if fast:
        beats[:] = [swap(last[0], core_pairs(n))]
    for k, name in enumerate(steps):
        later = set(steps[k:])
        held[:] = [a for a in (get() for get, uses in pinned.values() if later & set(uses)) if a is not None]
        tasks[name]()
    d_mixed, branch = box["d_mixed"], box["branch"]
    layer_out, grad_tokens, small = box["layer_out"], box["grad_tokens"], state["small"]
    sizes = [model, model, model, model, ff, model]
    if fast:
        cuts, at = [], 0
        for size in sizes:
            cuts.append(lax.dynamic_slice(state["small"], (0, at + device * (size // n)), (1, size // n)).reshape(size // n))
            at += size
    else:
        scatter = lambda g: lax.psum_scatter(g, AXES, scatter_dimension=0, tiled=True)
        factors = dict(qkv=(n1, d_mixed), proj=(att, branch), up=(n2, d_pre), down=(hidden, cot))
        grads = {k: scatter(dot_tn(*ab)) for k, ab in factors.items()}
        cuts, at = [], 0
        for size in sizes:
            cuts.append(scatter(small[0, at : at + size]))
            at += size
    shape = (rows, span, model)
    return (
        layer_out.reshape(shape), grad_tokens.reshape(shape), cuts[0], cuts[1], grads["qkv"], grads["proj"],
        cuts[2], cuts[3], grads["up"], cuts[4], grads["down"], cuts[5],
    )


def solution(mesh):
    wide, row, whole = P("rows", "seq", None), P(AXES), P()
    in_specs = (wide, P("rows", None), *[whole] * 10, wide)
    out_specs = (wide, wide, *[row] * 10)
    body = functools.partial(local, n_rows=mesh.shape["rows"], n_seq=mesh.shape["seq"])
    return jax.shard_map(body, mesh=mesh, in_specs=in_specs, out_specs=out_specs, check_vma=False)
```

```python
import functools

import jax
import jax.numpy as jnp
from jax import lax
from jax.experimental import pallas as pl
from jax.experimental.pallas import tpu as pltpu
from jax.sharding import PartitionSpec as P

HEADS = 16
EPS = 1e-05
BF, F32 = jnp.bfloat16, jnp.float32
AXES = ("rows", "seq")
DOWN = (1, 3)
STEPS = (
    "turn", "d1o", "d2o", "d1m", "dn2", "d2m", "n2t", "uo", "d1f", "mixer", "d1f", "merge", "um", "d2f",
    "layer", "d1f", "back", "q1o", "att", "d1f", "d2f", "d1a", "uf", "q1m", "q2o", "po", "d2f", "q2m",
    "pm", "dn1", "d2f", "q1f", "de", "small", "uf", "pf", "small", "q2f", "small", "uf", "pf", "small",
    "q1f", "small", "q2f", "small", "pf", "q1f", "q2f", "uf", "ue", "pf", "pe", "q2f", "q1f", "qe",
)
SUMS = 64
DEPTH = 80
TILE = 512
BEAT = 3


def dot(a, b):
    return jnp.dot(a, b, preferred_element_type=F32)


def dot_nt(a, b):
    return lax.dot_general(a, b, (((1,), (1,)), ((), ())), preferred_element_type=F32)


def dot_tn(a, b):
    return lax.dot_general(a, b, (((0,), (0,)), ((), ())), preferred_element_type=F32)


def iota(shape, dim):
    return lax.broadcasted_iota(jnp.int32, shape, dim)


SMEM = pl.BlockSpec(memory_space=pltpu.SMEM)
WHOLE = pl.BlockSpec(memory_space=pltpu.VMEM)
HBM = pl.BlockSpec(memory_space=pltpu.HBM)


def cut(at, size):
    return pl.ds(pl.multiple_of(at, size), size)


def in_vmem(x):
    return pltpu.with_memory_space_constraint(x, pltpu.VMEM)


def kernel_call(body, scalars, args, outs, scratch=(), far=(), hold=(), fetch=(), time=0.5, limit=4):
    n_in, n_hold, n_fetch, n_out = len(scalars) + len(args) + len(far), len(hold), len(fetch), len(outs)
    every = [(*o, True)[:3] for o in outs]
    every += [(f.shape, f.dtype, True) for f in fetch] + [((8, 128), F32, True)]

    def wrapped(*refs):
        ins, rest = refs[:n_in], refs[n_in + n_hold :]
        sources, rest = rest[:n_fetch], rest[n_fetch:]
        results, targets = rest[:n_out], rest[n_out : n_out + n_fetch]
        token, rest = rest[n_out + n_fetch], rest[n_out + n_fetch + 1 :]
        copies = []
        if n_fetch:
            sems, rest = rest[-1], rest[:-1]
            copies = [pltpu.make_async_copy(a, b, sems.at[k]) for k, (a, b) in enumerate(zip(sources, targets))]
        for copy in copies:
            copy.start()
        token[...] = jnp.zeros_like(token)
        body(*ins, *results, *rest)
        for copy in copies:
            copy.wait()

    shapes = [pltpu.VMEM(s, d) if v else jax.ShapeDtypeStruct(s, d) for s, d, v in every]
    in_hbm = lambda x: pltpu.with_memory_space_constraint(x, pltpu.HBM)
    out = pl.pallas_call(
        wrapped,
        name=body.__qualname__.split(".")[0],
        in_specs=[SMEM] * len(scalars)
        + [WHOLE] * len(args)
        + [HBM] * len(far)
        + [WHOLE] * n_hold
        + [HBM] * n_fetch,
        out_specs=[WHOLE] * len(every),
        out_shape=shapes,
        scratch_shapes=[*scratch, *([pltpu.SemaphoreType.DMA((n_fetch,))] if n_fetch else [])],
        compiler_params=pltpu.CompilerParams(vmem_limit_bytes=limit << 20),
        cost_estimate=pl.CostEstimate(flops=int(time * 1e10), bytes_accessed=1, transcendentals=0),
    )(*scalars, *map(in_vmem, args), *map(in_hbm, far), *map(in_vmem, hold), *map(in_hbm, fetch))
    return out


def normal(x):
    center = x - jnp.mean(x, -1, keepdims=True)
    root = lax.rsqrt(jnp.mean(center * center, -1, keepdims=True) + EPS)
    return center * root, root


def feature(u):
    return jnp.where(u > 0, u + 1.0, jnp.exp(jnp.minimum(u, 0.0)))


def keep_from(lb, row, span):
    last = 0 - span
    for k in range(lb.shape[1]):
        last = jnp.where(lb[row, k] < span, jnp.maximum(last, lb[row, k]), last)
    return last


def carry_to(lb, row, span):
    end = span
    for k in range(lb.shape[1]):
        end = jnp.where(lb[row, k] >= 0, jnp.minimum(end, lb[row, k]), end)
    return end


def block_mask(lb, row, span):
    t, s = iota((span, span), 0), iota((span, span), 1)
    ok = s <= t
    for k in range(lb.shape[1]):
        ok = ok & ((lb[row, k] > t) | (s >= lb[row, k]))
    return ok.astype(F32)


def pack_state(m):
    half = m.shape[0] // 2
    return jnp.where(iota((half, m.shape[1]), 1) < half, m[:half], m[half:])


def unpack_state(c):
    half = c.shape[0]
    left = iota(c.shape, 1) < half
    return jnp.concatenate([jnp.where(left, c, 0.0), jnp.where(left, 0.0, c)], 0)


def split(x):
    hi = x.astype(BF)
    return hi, (x - hi.astype(F32)).astype(BF)


def head_ones(lanes=128):
    half = lanes // 2
    return ((iota((lanes, lanes), 0) < half) == (iota((lanes, lanes), 1) < half)).astype(BF)


def head_sum(x):
    hi, lo = split(x)
    ones = head_ones(x.shape[1])
    return dot(jnp.concatenate([hi, lo], 1), jnp.concatenate([ones, ones], 0))


def dot_split(a, m):
    hi, lo = split(m)
    return dot(jnp.concatenate([a, a], 1), jnp.concatenate([hi, lo], 0))


def keys_values(lb, tokens, vectors, w_qkv, span, **kw):
    count, model = tokens.shape
    rows, width = count // span, 256
    n_vec, blocks = len(vectors), model // 512

    def body(lb, *refs):
        x_in, vec_in, w_in = refs[0], refs[1 : 1 + n_vec], refs[1 + n_vec]
        n1, km, v, own, *vecs = refs[2 + n_vec : 6 + 2 * n_vec]
        x, w, sems = refs[6 + 2 * n_vec :]

        def copy(k, a, b):
            return pltpu.make_async_copy(a, b, sems.at[k])

        def columns(j):
            lanes = slice(j * 512, (j + 1) * 512)
            return copy(1 + n_vec + j, w_in.at[:, model + j * 512 : model + (j + 1) * 512], w.at[:, lanes])

        head = [copy(0, x_in, x)] + [copy(1 + k, a, b) for k, (a, b) in enumerate(zip(vec_in, vecs))]
        for c in head:
            c.start()
        for c in [c for j in range(blocks) for c in (j, blocks + j)]:
            columns(c).start()
        for c in head:
            c.wait()

        @pl.loop(0, count // 64, unroll=2)
        def _(i):
            at = cut(i * 64, 64)
            n1[at] = (normal(x[at].astype(F32))[0] * vecs[0][...] + vecs[1][...]).astype(BF)

        kept = [iota((span, width), 0) >= keep_from(lb, r, span) for r in range(rows)]
        for j in range(model // width):
            if j * width % 512 == 0:
                columns(j * width // 512).wait()
                columns(blocks + j * width // 512).wait()
            lanes = slice(j * width, (j + 1) * width)
            key = feature(dot(n1[...], w[:, lanes])).astype(BF)
            val = dot(n1[...], w[:, model + j * width : model + (j + 1) * width]).astype(BF)
            km[:, lanes], v[:, lanes] = key, val
            for r in range(rows):
                part = slice(r * span, (r + 1) * span)
                owned = jnp.where(kept[r], key[part], jnp.zeros((), BF))
                for p in range(width // 128):
                    at = slice(p * 128, (p + 1) * 128)
                    block = j * (width // 128) + p
                    own[r, block, 0:SUMS] = pack_state(dot_tn(owned[:, at], val[part, at])).astype(BF)
                    total = jnp.sum(owned[:, at].astype(F32), 0, keepdims=True)
                    own[r, block, SUMS:DEPTH] = jnp.broadcast_to(total, (DEPTH - SUMS, 128)).astype(BF)

    wide = ((count, model), BF)
    outs = [wide, wide, wide, ((rows, model // 128, DEPTH, 128), BF)]
    outs += [(v.shape, v.dtype) for v in vectors]
    return kernel_call(
        body, (lb,), (), outs, far=(tokens, *vectors, w_qkv),
        scratch=[
            pltpu.VMEM((count, model), BF),
            pltpu.VMEM((model, 2 * model), BF),
            pltpu.SemaphoreType.DMA((1 + n_vec + 2 * blocks,)),
        ],
        limit=7, time=7.3, **kw,
    )


def merge_states(coefs, own, got, **kw):
    rows = own.shape[0]

    def body(c, a, b, out):
        for r in range(rows):
            out[r] = (c[0, r] * a[r].astype(F32) + c[1, r] * b[r].astype(F32)).astype(BF)

    return kernel_call(body, (coefs,), (own, got), [(own.shape, BF)], **kw)


def queries(normed, w_qkv, tables, shards, **kw):
    count, model = normed.shape
    tiles = model // TILE

    def body(tables, n, w_in, q, n_t, w, sems):
        copies = [
            pltpu.make_async_copy(w_in.at[:, j * TILE : (j + 1) * TILE], w.at[:, j * TILE : (j + 1) * TILE], sems.at[j])
            for j in range(tiles)
        ]
        for c in copies:
            c.start()
        turn(tables, n, n_t, model // shards)
        for j in range(tiles):
            lanes = slice(j * TILE, (j + 1) * TILE)
            copies[j].wait()
            q[:, lanes] = feature(dot(n[...], w[:, lanes])).astype(BF)

    return kernel_call(
        body, (tables,), (normed,), [((count, model), BF), ((model, count), BF)], far=(w_qkv,),
        scratch=[pltpu.VMEM((model, model), BF), pltpu.SemaphoreType.DMA((tiles,))],
        limit=5, time=3.9, **kw,
    )


def active_grads(cotangent, w_down, **kw):
    count, model = cotangent.shape
    ff = w_down.shape[0]

    def body(c, w, out):
        for j in range(ff // TILE):
            lanes = slice(j * TILE, (j + 1) * TILE)
            out[:, lanes] = dot_nt(c[...], w[lanes, :]).astype(BF)

    return kernel_call(
        body, (), (cotangent, w_down), [((count, ff), BF)], time=4.5, **kw
    )


def attend_inside(lb, query, key, values, span, **kw):
    count, model = query.shape
    rows = count // span

    def body(lb, q_ref, k_ref, v_ref, numer, denom, mask):
        for r in range(rows):
            mask[r] = block_mask(lb, r, span)
        left = iota((span, 128), 1) < 64
        zero = jnp.zeros((), BF)

        @pl.loop(0, model // 128, unroll=4)
        def _(p):
            lanes = cut(p * 128, 128)
            for r in range(rows):
                part = slice(r * span, (r + 1) * span)
                q, k, v = q_ref[part, lanes], k_ref[part, lanes], v_ref[part, lanes]
                total = 0.0
                for e in range(2):
                    mine = left if e == 0 else ~left
                    scores = dot_nt(jnp.where(mine, q, zero), k)
                    weights = (scores * mask[r]).astype(BF)
                    both = jnp.concatenate([jnp.where(mine, v, zero), mine.astype(BF)], 1)
                    total = total + dot(weights, both)
                numer[part, lanes] = total[:, :128]
                denom[part, lanes] = total[:, 128:]

    wide = ((count, model), F32)
    return kernel_call(
        body, (lb,), (query, key, values), [wide, wide],
        scratch=[pltpu.VMEM((rows, span, span), F32)], time=5.7, **kw,
    )


def state_of(coefs, gots, r, p):
    total = 0.0
    for i, got in enumerate(gots):
        total = total + coefs[i, r] * got[r, p].astype(F32)
    return total


def attend_join(lb, coefs, gots, query, numer, denom, tokens, w_proj, gain, bias, span, **kw):
    count, model = query.shape
    pairs, n = model // 128, len(gots)
    rows = count // span

    def body(lb, coefs, *refs):
        gots, (q_ref, num_ref, den_ref, x, w, g, b, att, rden, middle, n2) = refs[:n], refs[n:]
        place = iota((span, 128), 0)

        @pl.loop(0, pairs, unroll=4)
        def _(p):
            lanes = cut(p * 128, 128)
            for r in range(rows):
                part = slice(r * span, (r + 1) * span)
                state = state_of(coefs, gots, r, p)
                q = jnp.where(place < carry_to(lb, r, span), q_ref[part, lanes], jnp.zeros((), BF))
                num = num_ref[part, lanes] + dot_split(q, unpack_state(state[0:SUMS]))
                den = den_ref[part, lanes] + head_sum(q.astype(F32) * state[SUMS : SUMS + 1])
                inv = 1.0 / den
                rden[part, lanes] = inv
                att[part, lanes] = (num * inv).astype(BF)

        for j in range(model // 256):
            lanes = slice(j * 256, (j + 1) * 256)
            middle[:, lanes] = x[:, lanes].astype(F32) + dot(att[...], w[:, lanes])

        @pl.loop(0, count // 64, unroll=2)
        def _(i):
            at = cut(i * 64, 64)
            n2[at] = (normal(middle[at])[0] * g[...] + b[...]).astype(BF)

    wide = (count, model)
    return kernel_call(
        body, (lb, coefs), (*gots, query, numer, denom, tokens, w_proj, gain, bias),
        [(wide, BF), (wide, F32), (wide, F32), (wide, BF)],
        time=5.0, **kw,
    )


def expand(normed, w_up, up_bias, d_active, **kw):
    count, model = normed.shape
    ff = w_up.shape[1]
    c0, c1 = 0.7978845608028654, 0.7978845608028654 * 0.044715
    step = 32

    def body(n, w, b, da, hid, dp, total, even, odd):
        ones = jnp.ones((16, count), BF)

        def product(j, out):
            out[...] = dot(n[...], w[:, cut(j * TILE, TILE)])

        def rest(j, u_ref):
            lanes = cut(j * TILE, TILE)
            bias = b[:, lanes]
            for i in range(count // step):
                at = slice(i * step, (i + 1) * step)
                u = u_ref[at] + bias
                z = u * (c0 + c1 * (u * u))
                t = jnp.tanh(z)
                rise = 0.5 + 0.5 * t
                hid[at, lanes] = (u * rise).astype(BF)
                slope = rise * (1.0 + (1.0 - t) * (3.0 * z - (2.0 * c0) * u))
                dp[at, lanes] = (slope * da[at, lanes].astype(F32)).astype(BF)
            total[:, lanes] = dot(ones, dp[:, lanes])[0:1]

        tiles = ff // TILE
        product(0, even)

        @pl.loop(0, tiles // 2 - 1)
        def _(i):
            product(2 * i + 1, odd)
            rest(2 * i, even)
            product(2 * i + 2, even)
            rest(2 * i + 1, odd)

        product(tiles - 1, odd)
        rest(tiles - 2, even)
        rest(tiles - 1, odd)

    wide = ((count, ff), BF)
    return kernel_call(
        body, (), (normed, w_up, up_bias, d_active), [wide, wide, ((1, ff), F32)],
        scratch=[pltpu.VMEM((count, TILE), F32)] * 2, limit=6, time=11.0, **kw,
    )


def turn(tables, x, out, deep):
    for j in range(x.shape[1] // 128):
        t = x[:, j * 128 : (j + 1) * 128].T
        for k in range(128 // deep):
            out[cut(tables[2, j * (128 // deep) + k] * deep, deep), :] = t[k * deep : (k + 1) * deep]


def turned(x, tables, shards, **kw):
    count, model = x.shape
    deep = model // shards

    def body(tables, x, out):
        turn(tables, x, out, deep)

    return kernel_call(body, (tables,), (x,), [((model, count), BF)], **kw)


def weight_grad(lhs_t, rhs, first, steps, side, tables, got=None, **kw):
    deep, count = lhs_t.shape
    shards = tables.shape[1]
    rows, half = deep // shards, deep // 2
    time = 0.9 * steps
    shape = (deep, TILE * steps)

    def tile(b, which, j):
        return b[:, cut((which * side + first + j) * TILE, TILE)]

    if got is None:

        def body(tables, a, b, out):
            for j in range(steps):
                total = dot(a[...], tile(b, 1 - tables[3, 0], j)).astype(BF)
                for k in range(shards):
                    at = (k & 0b01010) | (k >> 4 & 1) << 2 | (k >> 2 & 1) << 4 | (~k & 1)
                    out[at * rows : (at + 1) * rows, j * TILE : (j + 1) * TILE] = total[k * rows : (k + 1) * rows]

        return kernel_call(body, (tables,), (lhs_t, rhs), [(shape, BF)], time=time, **kw)

    def body(tables, a, b, g, send, keep):
        for j in range(steps):
            lanes = slice(j * TILE, (j + 1) * TILE)
            total = dot(a[...], tile(b, tables[3, 0], j)) + g[:, lanes].astype(F32)
            send[:, lanes] = total[:half].astype(BF)
            keep[:, lanes] = total[half:].astype(BF)

    return kernel_call(
        body, (tables,), (lhs_t, rhs, got), [((half, TILE * steps), BF)] * 2, limit=9, time=time, **kw
    )


def transposed(x, **kw):
    def body(x, out):
        for j in range(x.shape[1] // TILE):
            out[j * TILE : (j + 1) * TILE, :] = x[:, j * TILE : (j + 1) * TILE].T

    return kernel_call(body, (), (x,), [(x.shape[::-1], x.dtype)], time=2.0, **kw)


def down_grad(hidden_t, cotangent, width, first, side, tables, got=None, **kw):
    ff, count = hidden_t.shape
    shards = tables.shape[1]
    deep = ff // shards
    per = TILE // deep
    steps = ff // TILE
    time = width / 110

    def product(tables, h, c, i, mine):
        which = 0 if mine else 1
        core = tables[3, 0]
        column = pl.multiple_of((core if mine else 1 - core) * side + first, 128)
        lhs = [h[cut(tables[which, per * i + k] * deep, deep), :] for k in range(per)]
        return dot(jnp.concatenate(lhs, 0), c[:, pl.ds(column, width)])

    if got is None:

        def body(tables, h, c, out):
            for i in range(steps):
                out[i * TILE : (i + 1) * TILE] = product(tables, h, c, i, False).astype(BF)

        return kernel_call(body, (tables,), (hidden_t, cotangent), [((ff, width), BF)], time=time, **kw)

    def body(tables, h, c, g, send, keep):
        for i in range(steps):
            total = product(tables, h, c, i, True) + g[i * TILE : (i + 1) * TILE].astype(F32)
            out, at = (send, i) if i < steps // 2 else (keep, i - steps // 2)
            out[at * TILE : (at + 1) * TILE] = total.astype(BF)

    return kernel_call(
        body, (tables,), (hidden_t, cotangent, got), [((ff // 2, width), BF)] * 2, limit=6, time=time, **kw
    )


def norm_grad_rows(e_ref, x_of, gain, count, write):
    step, model = 32, gain.shape[1]

    def one(i, sums):
        at = cut(i * step, step)
        e = e_ref[at]
        hat, root = normal(x_of(at))
        g = e * gain[...]
        back = root * (g - jnp.mean(g, -1, keepdims=True) - hat * jnp.mean(g * hat, -1, keepdims=True))
        write(at, back)
        eights = lambda v: jnp.sum(v.reshape(step // 8, 8, model), 0)
        return sums[0] + eights(e * hat), sums[1] + eights(e)

    zero = jnp.zeros((8, model), F32)
    sums = lax.fori_loop(0, count // step, one, (zero, zero), unroll=4)
    return [jnp.sum(s, 0, keepdims=True) for s in sums]


def second_norm_grads(d_pre, w_up, middle, cotangent, gain, **kw):
    count, ff = d_pre.shape
    model = w_up.shape[0]

    def body(d, w, mid, cot, g, d_mid, branch, g_gain, g_bias, g_down, e):
        for j in range(model // 256):
            lanes = slice(j * 256, (j + 1) * 256)
            e[:, lanes] = dot_nt(d[...], w[lanes, :])

        def write(at, back):
            out = cot[at].astype(F32) + back
            d_mid[at] = out
            branch[at] = out.astype(BF)

        g_gain[...], g_bias[...] = norm_grad_rows(e, lambda at: mid[at], g, count, write)
        g_down[...] = jnp.sum(cot[...].astype(F32), 0, keepdims=True)

    vec, wide = ((1, model), F32), (count, model)
    return kernel_call(
        body, (), (d_pre, w_up, middle, cotangent, gain), [(wide, F32), (wide, BF), vec, vec, vec],
        scratch=[pltpu.VMEM(wide, F32)], time=7.0, **kw,
    )


def mixer_grads(lb, branch, w_proj, attended, rden, query, span, **kw):
    count, model = branch.shape
    rows, pairs = count // span, model // 128

    def body(lb, br, w, att, rd, q_ref, dn, dd, own):
        place = iota((span, 128), 0)
        for j in range(model // 256):
            d_att = dot_nt(br[...], w[j * 256 : (j + 1) * 256, :])
            for k in range(2):
                p = 2 * j + k
                lanes = slice(p * 128, (p + 1) * 128)
                for r in range(rows):
                    part = slice(r * span, (r + 1) * span)
                    d, inv = d_att[part, k * 128 : (k + 1) * 128], rd[part, lanes]
                    d_den = -head_sum(d * att[part, lanes].astype(F32)) * inv
                    d_num = (d * inv).astype(BF)
                    dn[part, lanes], dd[part, lanes] = d_num, d_den
                    q = jnp.where(place < carry_to(lb, r, span), q_ref[part, lanes], jnp.zeros((), BF))
                    own[r, p, 0:SUMS] = pack_state(dot_tn(q, d_num)).astype(BF)
                    total = jnp.sum(d_den * q.astype(F32), 0, keepdims=True)
                    own[r, p, SUMS:DEPTH] = jnp.broadcast_to(total, (DEPTH - SUMS, 128)).astype(BF)

    wide = (count, model)
    return kernel_call(
        body, (lb,), (branch, w_proj, attended, rden, query),
        [(wide, BF), (wide, F32), ((rows, pairs, DEPTH, 128), BF)],
        time=5.0, **kw,
    )


def attend_back(lb, coefs, back_coefs, gots, back_gots, query, key, values, d_num, d_den, span, **kw):
    count, model = query.shape
    rows, n, m = count // span, len(gots), len(back_gots)

    def body(lb, coefs, back_coefs, *refs):
        gots, back_gots = refs[:n], refs[n : n + m]
        q_ref, k_ref, v_ref, dn_ref, dd_ref, out, mask, mask_t = refs[n + m :]
        for r in range(rows):
            ok = block_mask(lb, r, span)
            mask[r], mask_t[r] = ok, ok.T
        lane, place = iota((span, 128), 1), iota((span, 128), 0)
        left = lane < 64
        zero = jnp.zeros((), BF)

        @pl.loop(0, model // 128, unroll=4)
        def _(p):
            lanes = cut(p * 128, 128)
            for r in range(rows):
                part = slice(r * span, (r + 1) * span)
                carried = place < carry_to(lb, r, span)
                kept = place >= keep_from(lb, r, span)
                q, k, v = q_ref[part, lanes], k_ref[part, lanes], v_ref[part, lanes]
                dn, dd = dn_ref[part, lanes], dd_ref[part, lanes]
                hi, lo = split(dd)
                v_ones = jnp.concatenate([v, jnp.ones_like(v)], 1)
                dq = dk = dv = 0.0
                for e in range(2):
                    mine = left if e == 0 else ~left
                    at = 64 * e
                    qm, dnm = jnp.where(mine, q, zero), jnp.where(mine, dn, zero)
                    extra = jnp.where(lane == at, hi, jnp.where(lane == at + 1, lo, zero))
                    dn_den = jnp.concatenate([dnm, extra], 1)
                    ds = (dot_nt(dn_den, v_ones) * mask[r]).astype(BF)
                    w_t = (dot_nt(k, qm) * mask_t[r]).astype(BF)
                    dq = dq + dot(ds, jnp.where(mine, k, zero))
                    dk = dk + dot_tn(ds, qm)
                    dv = dv + dot(w_t, dnm)
                state, own = state_of(coefs, gots, r, p), state_of(back_coefs, back_gots, r, p)
                s_hi, s_lo = split(unpack_state(state[0:SUMS]))
                o_hi, o_lo = split(unpack_state(own[0:SUMS]))
                through_s = dot_nt(jnp.concatenate([dn, dn], 1), jnp.concatenate([s_hi, s_lo], 1))
                through_o = dot_nt(jnp.concatenate([v, v], 1), jnp.concatenate([o_hi, o_lo], 1))
                through_k = dot(jnp.concatenate([k, k], 1), jnp.concatenate([o_hi, o_lo], 0))
                dq = dq + jnp.where(carried, through_s + dd * state[SUMS : SUMS + 1], 0.0)
                dk = dk + jnp.where(kept, through_o + own[SUMS : SUMS + 1], 0.0)
                dv = dv + jnp.where(kept, through_k, 0.0)
                out[part, lanes] = (dq * jnp.minimum(q.astype(F32), 1.0)).astype(BF)
                out[part, cut(model + p * 128, 128)] = (dk * jnp.minimum(k.astype(F32), 1.0)).astype(BF)
                out[part, cut(2 * model + p * 128, 128)] = dv.astype(BF)

    return kernel_call(
        body, (lb, coefs, back_coefs), (*gots, *back_gots, query, key, values, d_num, d_den),
        [((count, 3 * model), BF)],
        scratch=[pltpu.VMEM((rows, span, span), F32)] * 2, time=12.0, **kw,
    )


def first_norm_grads(d_mixed, w_qkv, tokens, d_middle, gain, others, **kw):
    count = d_mixed.shape[0]
    model = w_qkv.shape[0]

    n = len(others)

    def body(d, x, dm, g, *refs):
        rest, (w_in, out, packed, e, w, sems) = refs[:n], refs[n:]
        tiles = model // 256

        def copy(j):
            return pltpu.make_async_copy(w_in.at[j * 256 : (j + 1) * 256, :], w.at[j % 2], sems.at[j % 2])

        copy(0).start()
        for j in range(tiles):
            copy(j).wait()
            if j + 1 < tiles:
                copy(j + 1).start()
            e[:, j * 256 : (j + 1) * 256] = dot_nt(d[...], w[j % 2])

        def write(at, back):
            out[at] = dm[at] + back

        at = 0
        for part in (*norm_grad_rows(e, lambda at: x[at].astype(F32), g, count, write), *[r[...] for r in rest]):
            packed[:, at : at + part.shape[1]] = part
            at += part.shape[1]

    wide, size = (count, model), 2 * model + sum(o.shape[1] for o in others)
    return kernel_call(
        body, (), (d_mixed, tokens, d_middle, gain, *others), [(wide, F32, False), ((1, size), F32)], far=(w_qkv,),
        scratch=[
            pltpu.VMEM(wide, F32), pltpu.VMEM((2, 256, w_qkv.shape[1]), BF), pltpu.SemaphoreType.DMA((2,))
        ], limit=10, time=6.5, **kw,
    )


def layer_result(hidden, w_down, middle, down_bias, **kw):
    count, ff = hidden.shape
    model, tiles = w_down.shape[1], 8
    deep = ff // tiles

    def body(h, mid, b, w_in, out, w, total, sems):
        def copy(j):
            return pltpu.make_async_copy(w_in.at[j * deep : (j + 1) * deep, :], w.at[j % 3], sems.at[j % 3])

        copy(0).start()
        copy(1).start()
        for j in range(tiles):
            copy(j).wait()
            if j + 2 < tiles:
                copy(j + 2).start()
            part = dot(h[:, j * deep : (j + 1) * deep], w[j % 3])
            if j == 0:
                total[...] = mid[...] + b[...] + part
            elif j < tiles - 1:
                total[...] += part
            else:
                out[...] = (total[...] + part).astype(BF)

    return kernel_call(
        body, (), (hidden, middle, down_bias), [((count, model), BF, False)], far=(w_down,),
        scratch=[pltpu.VMEM((3, deep, model), BF), pltpu.VMEM((count, model), F32), pltpu.SemaphoreType.DMA((3,))],
        time=5.5, limit=9, **kw,
    )


def swap(v, pairs):
    return lax.ppermute(v, AXES, pairs)


def state_plan(doc_end, n_rows, n_seq, later=False):
    me = lax.axis_index("seq")

    def reaches(a, b):
        def at(i):
            return lax.dynamic_index_in_dim(doc_end, i, 1, keepdims=False)

        return (at(a) == at(b)).astype(F32)

    pairs, merges, coefs = [], [], []
    size = 1
    while size < n_seq:
        step = [(r * n_seq + s, r * n_seq + (s ^ size)) for r in range(n_rows) for s in range(n_seq)]
        if 2 * size == n_seq:
            step = [p for p in step if bool(p[0] % n_seq & size) == later]
        pairs.append(step)
        upper = (me // size) % 2 == 1
        low = me // (2 * size) * (2 * size)
        mid, high = low + size, low + 2 * size
        if later:
            coefs.append(jnp.where(upper, 0.0, reaches(me + 1, mid)))
            same = reaches(low, mid)
            merges.append(jnp.stack([jnp.where(upper, same, 1.0), jnp.where(upper, 1.0, same)]))
        else:
            coefs.append(jnp.where(upper, reaches(mid, me), 0.0))
            same = reaches(mid, high)
            merges.append(jnp.stack([jnp.where(upper, 1.0, same), jnp.where(upper, same, 1.0)]))
        size *= 2
    return pairs, merges, jnp.stack(coefs)


def stage_pairs(n_rows, n_seq):
    def pairs(bit0, bit1):
        return [(i, i ^ (bit1 if i & 1 else bit0)) for i in range(n_rows * n_seq)]

    return [pairs(2, 4), pairs(8, 8), pairs(4, 2), pairs(16, 16)]


def core_pairs(n):
    return [(i, i ^ 1) for i in range(n)]


def shard_tables(device):
    j = jnp.arange(32, dtype=jnp.int32)

    def bits(device):
        core = device & 1
        return jnp.where(core == 0, 1, 2), 3, jnp.where(core == 0, 2, 1), 4, 0

    def order(device):
        move = 0
        for k, at in enumerate(bits(device)):
            move = move | (((31 - j) >> (4 - k)) & 1) << at
        return device ^ move

    place = 0
    for k, at in enumerate(bits(device)):
        place = place | (1 - (((j ^ device) >> at) & 1)) << (4 - k)
    return jnp.stack([order(device), order(device ^ 1), place, jnp.broadcast_to(device & 1, (32,))])


def fold(parts, **kw):
    rows = parts[0][0].shape[0]
    widths = [k.shape[1] for k, g in parts]
    half, step, n = rows // 2, min(32, rows // 2), len(parts)

    def body(*refs):
        send, keep = refs[2 * n :]

        @pl.loop(0, half // step, unroll=min(2, half // step))
        def _(i):
            at = 0
            top, low = cut(i * step, step), cut(half + i * step, step)
            for k, w in enumerate(widths):
                a, b = refs[2 * k], refs[2 * k + 1]
                lanes = slice(at, at + w)
                send[top, lanes] = (a[top].astype(F32) + b[top].astype(F32)).astype(BF)
                keep[top, lanes] = a[low].astype(F32) + b[low].astype(F32)
                at += w

    shape = (half, sum(widths))
    return kernel_call(body, (), [x for p in parts for x in p], [(shape, BF), (shape, F32)], **kw)


def place(tables, pieces, side, **kw):
    rows = pieces[0][0].shape[0]

    def body(tables, *refs):
        core, out = tables[3, 0], refs[-1]
        for k, (mine, got, at, w, to) in enumerate(pieces):
            out[:, pl.ds(pl.multiple_of(core * side + to, 128), w)] = refs[2 * k][:, at : at + w]
            out[:, pl.ds(pl.multiple_of((1 - core) * side + to, 128), w)] = refs[2 * k + 1][:, at : at + w].astype(F32)

    args = [x for p in pieces for x in p[:2]]
    return kernel_call(body, (tables,), args, [((rows, 2 * side), F32, False)], **kw)


def settle(a, **kw):
    def body(a, out):
        out[...] = a[...]

    return kernel_call(body, (), (a,), [(a.shape, a.dtype)], **kw)


def add(a, b, **kw):
    def body(a, b, out):
        out[...] = a[...] + b[...]

    return kernel_call(body, (), (a, b), [(a.shape, a.dtype)], **kw)


def local(
    tokens, bounds, norm1_gain, norm1_bias, w_qkv, w_proj, norm2_gain, norm2_bias,
    w_up, up_bias, w_down, down_bias, cotangent, n_rows, n_seq,
):
    rows, span, model = tokens.shape
    ff = w_up.shape[1]
    count, n = rows * span, n_rows * n_seq
    seq = lax.axis_index("seq")
    device = lax.axis_index("rows") * n_seq + seq
    core = device & 1
    lb = bounds - seq * span
    ends = jnp.arange(n_seq + 1, dtype=jnp.int32) * span - 1
    doc_end = jnp.sum((bounds[:, None, :] <= ends[None, :, None]).astype(jnp.int32), -1)
    x, cot = tokens.reshape(count, model), cotangent.reshape(count, model)
    vectors = [v.reshape(1, -1) for v in (norm1_gain, norm1_bias, norm2_gain, norm2_bias, up_bias, down_bias)]
    shards = 32
    fast = n == shards and model % (shards * 32) == 0 and ff % (shards * 128) == 0
    tables = shard_tables(device)
    plan = state_plan(doc_end, n_rows, n_seq)
    back_plan = state_plan(doc_end, n_rows, n_seq, later=True)
    held, last, ran, beats = [], [], [], []

    def run(kernel, *args, **kw):
        used = {id(x) for x in jax.tree.leaves(args)}
        small = kernel in (fold, settle, add, merge_states, turned)
        beat = beats and len(ran) % BEAT == 0 and "small" not in state
        extra = beats[:] if beat else []
        kept = [] if small else [x for x in held if id(x) not in used]
        *outs, token = kernel(*args, hold=kept + last + extra, **kw)
        last[:] = [token]
        ran.append(kernel)
        if beat:
            beats[:] = [swap(token, core_pairs(n))]
        return outs[0] if len(outs) == 1 else outs

    def keep(*arrays):
        held.extend(arrays)

    def drop(*arrays):
        held[:] = [x for x in held if all(x is not y for y in arrays)]

    def merged(plan, gots, own):
        return run(merge_states, plan[1][len(gots) - 1], own, gots[-1])

    n1, km, v, own, *vectors = run(keys_values, lb, x, vectors, w_qkv, span)
    gain1, bias1, gain2, bias2, b_up, b_down = vectors
    keep(gain1, gain2, bias2, b_up, b_down)
    gots = [swap(own, plan[0][0])]
    qm, n1_t = run(queries, n1, w_qkv, tables, shards)
    group = own
    for pairs in plan[0][1:]:
        group = merged(plan, gots, group)
        gots.append(swap(group, pairs))
    numer, denom, wdown_v, wproj_v, cot_v = run(attend_inside, lb, qm, km, v, span, fetch=(w_down, w_proj, cot))
    drop(km, v, qm)
    keep(numer, denom, wproj_v, cot_v)
    d_act = run(active_grads, cot_v, wdown_v)
    keep(d_act)
    att, rden, middle, n2, wup_v = run(
        attend_join, lb, plan[2], gots, qm, numer, denom, x, wproj_v, gain2, bias2, span, fetch=(w_up,)
    )
    drop(numer, denom, wproj_v)
    keep(wup_v, n2)
    hidden, d_pre, g_up_bias = run(expand, n2, wup_v, b_up, d_act)
    drop(d_act)
    keep(hidden, d_pre)

    stages = [*stage_pairs(n_rows, n_seq), core_pairs(n)] if fast else []
    state = {}

    def other(name, kernel, *args):
        if fast:
            out = run(kernel, *args, tables)
            state[name] = (kernel, args, swap(out, core_pairs(n)))

    def mine(name):
        if fast:
            kernel, args, got = state[name]
            send, kept = run(kernel, *args, tables, got)
            state[name] = (kept, swap(send, stages[0]), 1)

    def step(name, *names):
        if fast:
            parts = [state[k] for k in names or (name,)]
            send, kept = run(fold, [p[:2] for p in parts])
            at = parts[0][2]
            state[name] = (kept, swap(send, stages[at]), at + 1)

    def end(to, side, *pieces):
        if fast:
            found = []
            for name, w, column, at in pieces:
                kept, got, unused = state[name]
                found.append((kept, got, at, w, column))
            grads[to] = run(place, tables, found, side)

    def arrived(name):
        if fast:
            kept, got, at = state[name]
            state[name] = (kept, run(settle, got), at)

    grads, small_step, box = {}, [0], {}
    half = ff // TILE // 2
    widths = [w * model // 2 // sum(DOWN) for w in DOWN]

    def small_sum():
        k = small_step[0]
        if k:
            state["small"] = run(add, state["small"], state["small got"])
        if k < 5:
            state["small got"] = swap(state["small"], [(i, i ^ (1 << k)) for i in range(n)])
        small_step[0] += 1

    def second_norm():
        box["d_mid"], box["branch"], *box["sums"], box["w_proj"] = run(
            second_norm_grads, d_pre, wup_v, middle, cot_v, gain2, fetch=(w_proj,)
        )

    def mixer():
        box["d_num"], box["d_den"], box["group"] = run(
            mixer_grads, lb, box["branch"], box["w_proj"], att, rden, qm, span
        )
        box["gots"] = [swap(box["group"], back_plan[0][0])]

    def merge():
        for pairs in back_plan[0][1:]:
            box["group"] = merged(back_plan, box["gots"], box["group"])
            box["gots"].append(swap(box["group"], pairs))

    def back():
        box["d_mixed"] = run(
            attend_back, lb, plan[2], back_plan[2], gots, box["gots"], qm, km, v,
            box["d_num"], box["d_den"], span,
        )

    def first_norm():
        g_gain2, g_bias2, g_down_bias = box["sums"]
        others = [g_gain2, g_bias2, g_up_bias, g_down_bias]
        box["grad_tokens"], state["small"] = run(
            first_norm_grads, box["d_mixed"], w_qkv, x, box["d_mid"], gain1, others
        )

    def layer():
        box["layer_out"] = run(layer_result, hidden, w_down, middle, b_down)

    def keep_as(name, *call):
        box[name] = run(*call)

    def down(k):
        return down_grad, box["hidden_t"], cot_v, widths[k], sum(widths[:k]), model // 2

    tasks = dict(
        dn2=second_norm, mixer=mixer, merge=merge, layer=layer, back=back, dn1=first_norm, small=small_sum,
        turn=lambda: keep_as("hidden_t", transposed, hidden),
        n2t=lambda: keep_as("n2_t", turned, n2, tables, shards),
        att=lambda: keep_as("att_t", turned, att, tables, shards),
        d1o=lambda: other("d1", *down(0)),
        d2o=lambda: other("d2", *down(1)),
        uo=lambda: other("u", weight_grad, box["n2_t"], d_pre, 0, half, half),
        po=lambda: other("p", weight_grad, box["att_t"], box["branch"], 0, 1, 1),
        q1o=lambda: other("q1", weight_grad, n1_t, box["d_mixed"], 0, 2, 3),
        q2o=lambda: other("q2", weight_grad, n1_t, box["d_mixed"], 2, 1, 3),
        d1a=lambda: arrived("d1"),
        de=lambda: end("down", model // 2, ("d1", widths[0], 0, 0), ("d2", widths[1], widths[0], 0)),
        ue=lambda: end("up", ff // 2, ("u", ff // 2, 0, 0)),
        pe=lambda: end("proj", model // 2, ("p", TILE, 0, 0)),
        qe=lambda: end("qkv", 3 * TILE, ("q1", 2 * TILE, 0, 0), ("q2", TILE, 2 * TILE, 0)),
    )
    for name in ("d1", "d2", "u", "p", "q1", "q2"):
        tasks[name + "m"] = functools.partial(mine, name)
        tasks[name + "f"] = functools.partial(step, name)
    pinned = dict(
        hidden=(lambda: hidden, ("turn",)), d_pre=(lambda: d_pre, ("uo", "um", "dn2",)), cot=(lambda: cot_v, ("d1o", "d2o", "d1m", "d2m", "dn2",)),
        w_up=(lambda: wup_v, ("dn2",)), n2=(lambda: n2, ("n2t",)), hidden_t=(lambda: box.get("hidden_t"), ("d1o", "d2o", "d1m", "d2m",)),
        w_proj=(lambda: box.get("w_proj"), ("mixer",)),
        d_mixed=(lambda: box.get("d_mixed"), ("q1o", "q2o", "q1m", "q2m", "dn1",)), gain2=(lambda: gain2, ("dn2",)), b_down=(lambda: b_down, ("layer",)),
        gain1=(lambda: gain1, ("dn1",)),
    )
    local_steps = ("dn2", "mixer", "merge", "layer", "back", "dn1")
    steps = [name for name in STEPS if fast or name in local_steps]
    if fast:
        beats[:] = [swap(last[0], core_pairs(n))]
    for k, name in enumerate(steps):
        later = set(steps[k:])
        held[:] = [a for a in (get() for get, uses in pinned.values() if later & set(uses)) if a is not None]
        tasks[name]()
    d_mixed, branch = box["d_mixed"], box["branch"]
    layer_out, grad_tokens, small = box["layer_out"], box["grad_tokens"], state["small"]
    sizes = [model, model, model, model, ff, model]
    if fast:
        cuts, at = [], 0
        for size in sizes:
            cuts.append(lax.dynamic_slice(state["small"], (0, at + device * (size // n)), (1, size // n)).reshape(size // n))
            at += size
    else:
        scatter = lambda g: lax.psum_scatter(g, AXES, scatter_dimension=0, tiled=True)
        factors = dict(qkv=(n1, d_mixed), proj=(att, branch), up=(n2, d_pre), down=(hidden, cot))
        grads = {k: scatter(dot_tn(*ab)) for k, ab in factors.items()}
        cuts, at = [], 0
        for size in sizes:
            cuts.append(scatter(small[0, at : at + size]))
            at += size
    shape = (rows, span, model)
    return (
        layer_out.reshape(shape), grad_tokens.reshape(shape), cuts[0], cuts[1], grads["qkv"], grads["proj"],
        cuts[2], cuts[3], grads["up"], cuts[4], grads["down"], cuts[5],
    )


def solution(mesh):
    wide, row, whole = P("rows", "seq", None), P(AXES), P()
    in_specs = (wide, P("rows", None), *[whole] * 10, wide)
    out_specs = (wide, wide, *[row] * 10)
    body = functools.partial(local, n_rows=mesh.shape["rows"], n_seq=mesh.shape["seq"])
    return jax.shard_map(body, mesh=mesh, in_specs=in_specs, out_specs=out_specs, check_vma=False)
```
